32 devices in a mesh: guide: 2 (over x), seq: 8 (over z, core), blk: 2 (over y).
Axes of the slice: x: 2, y: 2, z: 4, core: 2. Of those that a mesh axis runs over, the one named last changes fastest.
Arguments:
- img_hidden: bfloat16 [2, 2, 512, 3072], P('guide', None, 'seq', 'blk'), may hold values from -6 to 6
- img_query: bfloat16 [2, 2, 512, 3072], P('guide', None, 'seq', 'blk')
- img_key: bfloat16 [2, 2, 512, 3072], P('guide', None, 'seq', 'blk')
- img_value: bfloat16 [2, 2, 512, 3072], P('guide', None, 'seq', 'blk'), may hold values from -6 to 6
- txt_key: bfloat16 [2, 2, 512, 3072], P('guide', None, 'seq', 'blk'), may hold values from -6 to 6
- txt_value: bfloat16 [2, 2, 512, 3072], P('guide', None, 'seq', 'blk'), may hold values from -6 to 6
- query_gain: float32 [128], replicated
- key_gain: float32 [2, 128], replicated
- gate: float32 [2, 2, 3072], P('guide', None, 'blk'), may hold values from -4 to 4
- proj_weight: bfloat16 [3072, 3072], P('blk'), may hold values from -0.15625 to 0.15625
- proj_bias: float32 [3072], P('blk'), may hold values from -3 to 3
- guidance: float32 [2], replicated, may hold values from 1.5 to 5
- text_len: int32 [2], replicated, may hold values from 1 to 512, as said below
- step_index: int32 [1], replicated, may hold values from 0 to 7
- latent: bfloat16 [2, 512, 3072], P('guide', 'seq', 'blk'), may hold values from -6 to 6
Outputs:
- guided: bfloat16 [2, 512, 3072], P('guide', 'seq', 'blk')
- next_state: bfloat16 [2, 512, 3072], P('guide', 'seq', 'blk')
The draws below stay inside these ranges and needn't reach their ends.
Inputs may be any that keep to these rules, and one draw needn't show every extreme that they name: `text_len`: some prompt has all 512 text slots live.
All inputs are finite; a program needn't handle non-finite values.
Results may differ from the reference program's by a relative error of at most 0.0095.
Values may be sent and summed in bfloat16 or wider, within the bound.
A program may use at most 64 MiB of HBM per device.

```python
import jax
import jax.numpy as jnp
from jax import lax

D = 3072
HEADS = 24
HD = 128
GRID = 64
PROMPTS = 2
STEPS = 8
TXT = 512
IMG = 512


def draw_query_gain(key, part):
    return 1.0 + jax.random.uniform(jax.random.fold_in(key, 11), (HD,), jnp.float32, -0.4, 0.4)


def draw_key_gain(key, part):
    return 1.0 + jax.random.uniform(jax.random.fold_in(key, 12), (2, HD), jnp.float32, -0.4, 0.4)


def draw_img_query(key, part):
    return jnp.clip(jax.random.normal(jax.random.fold_in(key, 31), (2, PROMPTS, IMG, D), jnp.float32), -6.0, 6.0).astype(jnp.bfloat16)


def draw_img_key(key, part):
    return jnp.clip(jax.random.normal(jax.random.fold_in(key, 32), (2, PROMPTS, IMG, D), jnp.float32), -6.0, 6.0).astype(jnp.bfloat16)


def draw_text_len(key, part):
    lengths = jax.random.randint(jax.random.fold_in(key, 41), (PROMPTS,), 1, TXT + 1)
    pick = jax.random.randint(jax.random.fold_in(key, 42), (), 0, PROMPTS)
    return jnp.where(jnp.arange(PROMPTS) == pick, TXT, lengths).astype(jnp.int32)


def raised(array, own_key, source, target, blocks, factor):
    def block_of(axis_at):
        return (jnp.arange(array.shape[axis_at]) // (array.shape[axis_at] // blocks)).reshape((-1,) + (1,) * (array.ndim - 1 - axis_at))

    near = jax.random.permutation(own_key, blocks)[block_of(target)]
    far = (block_of(target) + blocks // 2) % blocks
    return jnp.where((block_of(source) == near) | (block_of(source) == far), factor * array, array)


def steps_of(own_key, shape, split, low, high):
    gain, own = 1.0, jax.random.fold_in(own_key, 6)
    for position, blocks in split:
        draws = jnp.exp(jax.random.uniform(jax.random.fold_in(own, position), (blocks,), jnp.float32, low / len(split), high / len(split)))
        gain = gain * jnp.repeat(draws, shape[position] // blocks).reshape([-1 if axis == position else 1 for axis in range(len(shape))])
    return gain


def gaussian(rng, dims, deviation, most, cuts=(), held_as=jnp.bfloat16):
    entries = jax.random.normal(rng, dims, jnp.float32) * deviation
    if len(cuts) > 0:
        entries = steps_of(rng, dims, cuts, -0.22, 0.18) * entries
    return jnp.clip(entries, min=-most, max=most).astype(held_as)


def noise_with(own_key, extent, width, limit, split, heavy, dtype=jnp.bfloat16):
    array = width * jax.random.normal(own_key, extent, jnp.float32)
    if split:
        array = array * steps_of(own_key, extent, split, -0.22, 0.18)
    return jnp.clip(raised(array, jax.random.fold_in(own_key, 3), *heavy), -limit, limit).astype(dtype)


def setup_inputs(seed: int = 0) -> dict:
    streams_of = jax.random.split(jax.random.key(seed), 16)
    return {
        "img_hidden": gaussian(streams_of[0], (2, PROMPTS, IMG, D), 1.0, 6.0, ((0, 2), (2, 8), (3, 2))),
        "img_query": draw_img_query(jax.random.fold_in(streams_of[15], 71), 0),
        "img_key": draw_img_key(jax.random.fold_in(streams_of[15], 71), 0),
        "img_value": gaussian(streams_of[3], (2, PROMPTS, IMG, D), 1.0, 6.0, ((0, 2), (2, 8), (3, 2))),
        "txt_key": gaussian(streams_of[4], (2, PROMPTS, TXT, D), 1.0, 6.0, ((0, 2), (2, 8), (3, 2))),
        "txt_value": gaussian(streams_of[5], (2, PROMPTS, TXT, D), 1.0, 6.0, ((0, 2), (2, 8), (3, 2))),
        "query_gain": draw_query_gain(jax.random.fold_in(streams_of[15], 71), 0),
        "key_gain": draw_key_gain(jax.random.fold_in(streams_of[15], 71), 0),
        "gate": gaussian(streams_of[8], (2, PROMPTS, D), 1.0, 4.0, ((0, 2), (2, 2)), jnp.float32),
        "proj_weight": noise_with(streams_of[9], (D, D), D ** -0.5, 0.15625, ((0, 2),), (0, 1, 2, 2.0)),
        "proj_bias": gaussian(streams_of[10], (D,), 0.5, 3.0, ((0, 2),), jnp.float32),
        "guidance": jnp.clip(jax.random.uniform(streams_of[11], (PROMPTS,), jnp.float32, 1.5, 5.0), 1.5, 5.0),
        "text_len": draw_text_len(jax.random.fold_in(streams_of[15], 71), 0),
        "step_index": jax.random.randint(streams_of[13], (1,), 0, STEPS).astype(jnp.int32),
        "latent": gaussian(streams_of[14], (PROMPTS, IMG, D), 1.0, 6.0, ((0, 2), (1, 8), (2, 2))),
    }


def rope_angles(positions):
    first = HD // 8
    second = (HD - first) // 2
    freqs = 10000.0 ** (-jnp.arange(0, second, 2).astype(jnp.float32) / second)
    rows = (positions // GRID).astype(jnp.float32)
    cols = (positions % GRID).astype(jnp.float32)
    zeros = jnp.zeros((positions.shape[0], first // 2), jnp.float32)
    return jnp.concatenate([zeros, rows[:, None] * freqs, cols[:, None] * freqs], -1)

def rotate(values, angles):
    pairs = values.reshape(values.shape[:-1] + (HD // 2, 2))
    cosine = jnp.cos(angles)[:, None, :]
    sine = jnp.sin(angles)[:, None, :]
    first = pairs[..., 0] * cosine - pairs[..., 1] * sine
    second = pairs[..., 0] * sine + pairs[..., 1] * cosine
    return jnp.stack([first, second], -1).reshape(values.shape)

def normed(values, gain_row):
    heads = values.astype(jnp.float32).reshape(values.shape[0], HEADS, HD)
    return heads / jnp.sqrt(lax.optimization_barrier(jnp.mean(heads * heads, -1, keepdims=True)) + 1e-06) * gain_row

def one_half(hidden, query, key_img, value_img, key_txt, value_txt, query_gain, key_gain, gate_row, proj_weight, proj_bias, length):
    angles = rope_angles(jnp.arange(IMG))
    queries = rotate(normed(query, query_gain), angles).astype(jnp.bfloat16)
    keys_img = rotate(normed(key_img, key_gain[0]), angles).astype(jnp.bfloat16)
    keys_txt = normed(key_txt, key_gain[1]).astype(jnp.bfloat16)
    keys = jnp.concatenate([keys_txt, keys_img], 0)
    values = jnp.concatenate([value_txt, value_img], 0).reshape(TXT + IMG, HEADS, HD)
    live = jnp.concatenate([jnp.arange(TXT) < length, jnp.ones((IMG,), bool)])
    scores = jnp.einsum('qhd,khd->hqk', queries.astype(jnp.float32), keys.astype(jnp.float32)) * HD ** (-0.5)
    scores = jnp.where(live[None, None, :], scores, -1e+30)
    top = lax.optimization_barrier(jnp.max(scores, -1, keepdims=True))
    expo = jnp.exp(scores - top)
    total = lax.optimization_barrier(jnp.sum(expo, -1))
    weights = expo.astype(jnp.bfloat16)
    attn = jnp.einsum('hqk,khd->qhd', weights.astype(jnp.float32), values.astype(jnp.float32))
    attn = (attn / jnp.transpose(total)[:, :, None]).astype(jnp.bfloat16).reshape(IMG, D)
    proj = jnp.dot(attn, proj_weight, preferred_element_type=jnp.float32) + proj_bias
    return (hidden.astype(jnp.float32) + gate_row * proj).astype(jnp.bfloat16)

def plan(index):
    u_now = 1.0 - index.astype(jnp.float32) / STEPS
    u_next = 1.0 - (index + 1).astype(jnp.float32) / STEPS
    return 3.0 * u_next / (1.0 + 2.0 * u_next) - 3.0 * u_now / (1.0 + 2.0 * u_now)

def reference(img_hidden, img_query, img_key, img_value, txt_key, txt_value, query_gain, key_gain, gate, proj_weight, proj_bias, guidance, text_len, step_index, latent):
    step_size = plan(step_index[0])
    guided_rows = []
    next_rows = []
    for prompt in range(PROMPTS):
        outs = []
        for half in range(2):
            outs.append(one_half(img_hidden[half, prompt], img_query[half, prompt], img_key[half, prompt], img_value[half, prompt], txt_key[half, prompt], txt_value[half, prompt], query_gain, key_gain, gate[half, prompt], proj_weight, proj_bias, text_len[prompt]))
        cond = outs[0].astype(jnp.float32)
        uncond = outs[1].astype(jnp.float32)
        guided_f = uncond + guidance[prompt] * (cond - uncond)
        guided_rows.append(guided_f.astype(jnp.bfloat16))
        next_rows.append((latent[prompt].astype(jnp.float32) + step_size * guided_f).astype(jnp.bfloat16))
    return (jnp.stack(guided_rows, 0), jnp.stack(next_rows, 0))
```

```python
import jax
import jax.numpy as jnp
import numpy as np
from jax import lax
from jax.experimental import pallas as pl
from jax.experimental.pallas import tpu as pltpu
from jax.sharding import PartitionSpec as P

HD = 128
GRID = 64
STEPS = 8


def rope_angles(positions):
    first = HD // 8
    second = (HD - first) // 2
    freqs = 10000.0 ** (-jnp.arange(0, second, 2).astype(jnp.float32) / second)
    rows = (positions // GRID).astype(jnp.float32)
    cols = (positions % GRID).astype(jnp.float32)
    zeros = jnp.zeros((positions.shape[0], first // 2), jnp.float32)
    return jnp.concatenate([zeros, rows[:, None] * freqs, cols[:, None] * freqs], -1)


def rotate(values, angles):
    pairs = values.reshape(values.shape[:-1] + (HD // 2, 2))
    cosine = jnp.cos(angles)[None, :, None, :]
    sine = jnp.sin(angles)[None, :, None, :]
    first = pairs[..., 0] * cosine - pairs[..., 1] * sine
    second = pairs[..., 0] * sine + pairs[..., 1] * cosine
    return jnp.stack([first, second], -1).reshape(values.shape)


def normed(values, gain_row):
    heads = values.astype(jnp.float32).reshape(
        values.shape[0], values.shape[1], values.shape[2] // HD, HD
    )
    return heads / jnp.sqrt(jnp.mean(heads * heads, -1, keepdims=True) + 1e-06) * gain_row


def shards(
    img_hidden,
    img_query,
    img_key,
    img_value,
    txt_key,
    txt_value,
    query_gain,
    key_gain,
    gate,
    proj_weight,
    proj_bias,
    guidance,
    text_len,
    step_index,
    latent,
):
    prompts = img_query.shape[1]
    img_here = img_query.shape[2]
    txt_here = txt_key.shape[2]
    width_here = img_query.shape[3]
    heads_here = width_here // HD
    slot_here = img_here + txt_here
    positions = lax.axis_index("seq") * img_here + jnp.arange(img_here)
    angles = rope_angles(positions)
    queries = rotate(normed(img_query[0], query_gain), angles).astype(jnp.bfloat16)
    keys_img = rotate(normed(img_key[0], key_gain[0]), angles).astype(jnp.bfloat16)
    keys_txt = normed(txt_key[0], key_gain[1]).astype(jnp.bfloat16)
    keys_local = jnp.concatenate([keys_txt, keys_img], 1).reshape(prompts, slot_here, width_here)
    values_local = jnp.concatenate([txt_value[0], img_value[0]], 1)
    running = jnp.full((prompts, img_here, heads_here), -1e30, jnp.float32)
    key_piece = lax.all_gather(keys_local, "seq", axis=1, tiled=True)
    value_piece = lax.all_gather(values_local, "seq", axis=1, tiled=True)
    count = key_piece.shape[1]
    index = jnp.arange(count)
    device = index // slot_here
    within = index % slot_here
    text_pos = device * txt_here + within
    live = (within >= txt_here)[None, :] | (text_pos[None, :] < text_len[:, None])
    key_heads = key_piece.reshape(prompts, count, heads_here, HD)
    value_heads = value_piece.reshape(prompts, count, heads_here, HD)
    scores = jnp.einsum(
        "pqhd,pkhd->pqhk", queries, key_heads, preferred_element_type=jnp.float32
    ) * HD ** (-0.5)
    mask = live[:, None, None, :]
    scores = jnp.where(mask, scores, -1e30)
    newest = jnp.maximum(running, jnp.max(scores, -1))
    expo = jnp.where(mask, jnp.exp(scores - newest[..., None]), 0.0)
    total = jnp.sum(expo, -1)
    accum = jnp.einsum(
        "pqhk,pkhd->pqhd",
        expo.astype(jnp.bfloat16),
        value_heads,
        preferred_element_type=jnp.float32,
    )
    running, total, accum = (newest, total, accum)
    attn = (accum / total[..., None]).astype(jnp.bfloat16).reshape(prompts * img_here, width_here)
    partial_value = jnp.dot(attn, proj_weight, preferred_element_type=jnp.float32)
    proj = lax.psum_scatter(
        partial_value.astype(jnp.bfloat16), "blk", scatter_dimension=1, tiled=True
    ).astype(jnp.float32)
    proj = (proj + proj_bias).reshape(prompts, img_here, width_here)
    layer_out = (img_hidden[0].astype(jnp.float32) + gate[0][:, None, :] * proj).astype(
        jnp.bfloat16
    )
    both_halves = lax.all_to_all(layer_out[None], "guide", split_axis=1, concat_axis=0, tiled=True)
    cond = both_halves[0].astype(jnp.float32)
    uncond = both_halves[1].astype(jnp.float32)
    own_prompts = cond.shape[0]
    scale_here = lax.dynamic_slice_in_dim(
        guidance, lax.axis_index("guide") * own_prompts, own_prompts, 0
    )
    guided_f = uncond + scale_here[:, None, None] * (cond - uncond)
    index = step_index[0]
    u_now = 1.0 - index.astype(jnp.float32) / STEPS
    u_next = 1.0 - (index + 1).astype(jnp.float32) / STEPS
    step_size = 3.0 * u_next / (1.0 + 2.0 * u_next) - 3.0 * u_now / (1.0 + 2.0 * u_now)
    next_state = (latent.astype(jnp.float32) + step_size * guided_f).astype(jnp.bfloat16)
    return (guided_f.astype(jnp.bfloat16), next_state)


CHIPS = 4
ROWS = 64
CHUNKS = 4
PER = 3
UNITS = CHUNKS * PER
HEADS_CORE = 6
SCALE = HD ** (-0.5)
F32 = jnp.float32
BF16 = jnp.bfloat16


def rope_table(devices):
    first = HD // 8
    second = (HD - first) // 2
    freqs = (10000.0 ** (-np.arange(0, second, 2).astype(np.float32) / second)).astype(np.float32)
    positions = np.arange(devices * ROWS)
    rows = (positions // GRID).astype(np.float32)[:, None] * freqs
    cols = (positions % GRID).astype(np.float32)[:, None] * freqs
    angles = np.concatenate([np.zeros((positions.size, first // 2), np.float32), rows, cols], -1)
    angles = np.repeat(angles, 2, -1)
    table = np.concatenate([np.cos(angles), np.sin(angles)], -1).astype(np.float32)
    return table.reshape(devices, ROWS, 2 * HD)


def swap_matrix():
    out = np.zeros((HD, HD), np.float32)
    for pair in range(HD // 2):
        out[2 * pair + 1, 2 * pair] = -1.0
        out[2 * pair, 2 * pair + 1] = 1.0
    return out


def step_sizes():
    def sigma(i):
        u = 1.0 - i / STEPS
        return 3.0 * u / (1.0 + 2.0 * u)

    return [sigma(i + 1) - sigma(i) for i in range(STEPS)]


def fused(
    hid, q_in, ki_in, vi_in, kt_in, vt_in, qg, kg, gate, w_hbm, bias, guidance, tlen, sidx, latent,
    rope_hbm, perm, guided_o, next_o,
    weight, rope, q_all, keys, vals, vals_t, stage_q, stage_kv, part, lse, in_part, in_lse,
    out_part, out_lse, own_t, attn, y_out, y_in, proj, x_out, x_in,
    w_sem, rope_sem, ex_send, ex_recv, q_send, q_recv, p_send, p_recv, s_send, s_recv,
    a_send, a_recv, y_send, y_recv, x_send, x_recv,
):
    g = lax.axis_index("guide")
    s = lax.axis_index("seq")
    b = lax.axis_index("blk")
    z = s // 2
    core = s % 2
    other = 1 - core
    peer = {"seq": 2 * z + other}
    left = {"seq": s - 2}
    right = {"seq": s + 2}
    y_peer = {"blk": 1 - b}
    x_peer = {"guide": 1 - g}
    width = weight.shape[0]
    half = width // 2
    last = CHIPS - 1

    def prompt_of(order):
        return (1 - g) * (1 - order) + g * order

    def remote(src, dst, send, recv, device):
        return pltpu.make_async_remote_copy(
            src_ref=src, dst_ref=dst, send_sem=send, recv_sem=recv,
            device_id=device, device_id_type=pl.DeviceIdType.MESH,
        )

    barrier = pltpu.get_barrier_semaphore()

    def greet(device):
        pl.semaphore_signal(barrier, inc=1, device_id=device, device_id_type=pl.DeviceIdType.MESH)

    greet(peer)
    greet(y_peer)
    greet(x_peer)
    pl.when(z > 0)(lambda: greet(left))
    pl.when(z < last)(lambda: greet(right))

    w_copy = pltpu.make_async_copy(w_hbm, weight, w_sem)
    w_copy.start()
    rope_copy = pltpu.make_async_copy(rope_hbm.at[s], rope, rope_sem)
    rope_copy.start()
    rope_copy.wait()

    lane = lax.broadcasted_iota(jnp.int32, (8, HD), 1)

    def swapped(row):
        wide = jnp.broadcast_to(row, (8, HD))
        return jnp.where(
            lane % 2 == 0, pltpu.roll(wide, HD - 1, 1), pltpu.roll(wide, 1, 1)
        )[0:1]

    def scaled(values):
        return lax.rsqrt(jnp.mean(values * values, -1, keepdims=True) + 1e-06)

    def roped(values, gain):
        wide = values.astype(F32)
        turned = jnp.dot(values, perm[...], preferred_element_type=F32)
        cosine = rope[:, :HD] * gain
        sine = rope[:, HD:] * swapped(gain)
        return (scaled(wide) * (wide * cosine + turned * sine)).astype(BF16)

    def plain(values, gain):
        wide = values.astype(F32)
        return (wide * scaled(wide) * gain).astype(BF16)

    def each_chunk(step):
        def run(chunk, carry):
            step(chunk)
            return carry

        lax.fori_loop(0, CHUNKS, run, 0)

    def place(chunk, i, owner):
        order = chunk // 2
        head = owner * HEADS_CORE + (chunk % 2) * PER + i
        return prompt_of(order), pl.ds(pl.multiple_of(head * HD, HD), HD)

    mine = pl.ds(pl.multiple_of(core * ROWS, ROWS), ROWS)
    mine_img = pl.ds(pl.multiple_of((2 + core) * ROWS, ROWS), ROWS)
    theirs = pl.ds(pl.multiple_of(other * ROWS, ROWS), ROWS)
    theirs_img = pl.ds(pl.multiple_of((2 + other) * ROWS, ROWS), ROWS)

    def queries_for_peer(chunk):
        for i in range(PER):
            p, cols = place(chunk, i, other)
            stage_q[chunk * PER + i] = roped(q_in[0, p, :, cols], qg[...])

    def queries_own(chunk):
        for i in range(PER):
            p, cols = place(chunk, i, core)
            q_all[z, chunk * PER + i, mine, :] = roped(q_in[0, p, :, cols], qg[...])

    def kv_for_peer(chunk):
        for i in range(PER):
            p, cols = place(chunk, i, other)
            unit = chunk * PER + i
            stage_kv[0, unit] = plain(kt_in[0, p, :, cols], kg[1:2])
            stage_kv[1, unit] = roped(ki_in[0, p, :, cols], kg[0:1])
            stage_kv[2, unit] = vt_in[0, p, :, cols]
            stage_kv[3, unit] = vi_in[0, p, :, cols]

    def kv_own(chunk):
        for i in range(PER):
            p, cols = place(chunk, i, core)
            unit = chunk * PER + i
            keys[unit, mine, :] = plain(kt_in[0, p, :, cols], kg[1:2])
            keys[unit, mine_img, :] = roped(ki_in[0, p, :, cols], kg[0:1])
            vals[unit, mine, :] = vt_in[0, p, :, cols]
            vals[unit, mine_img, :] = vi_in[0, p, :, cols]

    def exchange(sending):
        rows, rows_img = (mine, mine_img) if sending else (theirs, theirs_img)
        pairs = [
            (stage_q, q_all.at[z, :, rows, :]),
            (stage_kv.at[0], keys.at[:, rows, :]),
            (stage_kv.at[1], keys.at[:, rows_img, :]),
            (stage_kv.at[2], vals.at[:, rows, :]),
            (stage_kv.at[3], vals.at[:, rows_img, :]),
        ]
        return [
            remote(src, dst, ex_send.at[n], ex_recv.at[n], peer)
            for n, (src, dst) in enumerate(pairs)
        ]

    def some(chunk):
        return pl.ds(chunk * PER, PER)

    def query_copy(to_right, owner, chunk):
        block = q_all.at[owner, some(chunk)]
        way = 1 if to_right else 0
        return remote(
            block, block, q_send.at[way, owner, chunk], q_recv.at[owner, chunk],
            right if to_right else left,
        )

    def part_copies(to_right, owner, chunk):
        way = 0 if to_right else 1
        device = right if to_right else left
        return (
            remote(
                out_part.at[owner, some(chunk)], in_part.at[way, owner, some(chunk)],
                p_send.at[owner, chunk], p_recv.at[way, owner, chunk], device,
            ),
            remote(
                out_lse.at[owner, chunk], in_lse.at[way, owner, chunk],
                s_send.at[owner, chunk], s_recv.at[way, owner, chunk], device,
            ),
        )

    def attend(owner, chunk):
        live_text = tlen[prompt_of(chunk // 2)]
        row = lax.broadcasted_iota(jnp.int32, (4 * ROWS, HD), 0)
        live = (row >= 2 * ROWS) | (row + z * (2 * ROWS) < live_text)
        for i in range(PER):
            unit = chunk * PER + i
            scores = lax.dot_general(
                keys[unit], q_all[owner, unit], (((1,), (1,)), ((), ())),
                preferred_element_type=F32,
            ) * SCALE
            scores = jnp.where(live, scores, -1e30)
            top = jnp.max(scores, 0, keepdims=True)
            expo = jnp.exp(scores - top)
            total = jnp.sum(expo, 0, keepdims=True)
            out = jnp.dot(vals_t[unit], expo.astype(BF16), preferred_element_type=F32)
            part[owner, unit] = out / total
            lse[owner, chunk, i : i + 1, :] = top + jnp.log(total)

    def absorb(way, owner, chunk):
        for copy in part_copies(way == 0, owner, chunk):
            copy.wait_recv()
        for i in range(PER):
            unit = chunk * PER + i
            here = lse[owner, chunk, i : i + 1, :]
            there = in_lse[way, owner, chunk, i : i + 1, :]
            top = jnp.maximum(here, there)
            w_here = jnp.exp(here - top)
            w_there = jnp.exp(there - top)
            total = w_here + w_there
            part[owner, unit] = part[owner, unit] * (w_here / total) + in_part[
                way, owner, unit
            ].astype(F32) * (w_there / total)
            lse[owner, chunk, i : i + 1, :] = top + jnp.log(total)

    def relay(to_right, owner, chunk):
        if to_right:
            pl.when(z > 0)(lambda: absorb(0, owner, chunk))
        else:
            pl.when(z < last)(lambda: absorb(1, owner, chunk))
        out_part[owner, some(chunk)] = part[owner, some(chunk)].astype(BF16)
        out_lse[owner, chunk] = lse[owner, chunk]
        for copy in part_copies(to_right, owner, chunk):
            copy.start()

    def from_left(owner, chunk):
        query_copy(True, owner, chunk).wait_recv()
        pl.when(z < last)(lambda: query_copy(True, owner, chunk).start())

    def from_right(owner, chunk):
        query_copy(False, owner, chunk).wait_recv()
        pl.when(z > 0)(lambda: query_copy(False, owner, chunk).start())

    def attn_copy(chunk, sending):
        first = (core if sending else other) * HEADS_CORE + (chunk % 2) * PER
        return remote(
            own_t.at[some(chunk), theirs, :], attn.at[chunk // 2, pl.ds(first, PER)],
            a_send.at[chunk], a_recv.at[chunk], peer,
        )

    def conclude(chunk):
        pl.when(z > 0)(lambda: absorb(0, z, chunk))
        pl.when(z < last)(lambda: absorb(1, z, chunk))
        for i in range(PER):
            own_t[chunk * PER + i] = part[z, chunk * PER + i].T.astype(BF16)
        attn_copy(chunk, True).start()
        attn[chunk // 2, pl.ds(core * HEADS_CORE + (chunk % 2) * PER, PER)] = own_t[
            some(chunk), mine, :
        ]

    tile = 256

    def product(order, column):
        rows = jnp.concatenate([attn[order, h] for h in range(2 * HEADS_CORE)], -1)
        return jnp.dot(
            rows, weight[:, pl.ds(pl.multiple_of(column, tile), tile)],
            preferred_element_type=F32,
        )

    def y_copy(order, n):
        return remote(
            y_out.at[order, n], y_in.at[order, n], y_send.at[order, n], y_recv.at[order, n], y_peer
        )

    def project(order):
        for chunk in (2 * order, 2 * order + 1):
            attn_copy(chunk, False).wait_recv()
        for n in range(2):
            def send_tile(at, carry, n=n):
                start = pl.multiple_of(at * tile, tile)
                y_out[order, n, :, pl.ds(start, tile)] = product(
                    order, (1 - b) * width + n * half + start
                ).astype(BF16)
                return carry

            lax.fori_loop(0, half // tile, send_tile, 0)
            y_copy(order, n).start()

        def own_tile(at, carry):
            start = pl.multiple_of(at * tile, tile)
            proj[order, :, pl.ds(start, tile)] = product(order, b * width + start)
            return carry

        lax.fori_loop(0, width // tile, own_tile, 0)

    def x_copy(n):
        return remote(x_out.at[n], x_in.at[n], x_send.at[n], x_recv.at[n], x_peer)

    def layer(order, n):
        y_copy(order, n).wait_recv()
        p = prompt_of(order)
        cols = pl.ds(n * half, half)
        summed = proj[order, :, cols] + y_in[order, n].astype(F32) + bias[:, cols]
        return (
            hid[0, p, :, cols].astype(F32) + gate[0, pl.ds(p, 1), cols] * summed
        ).astype(BF16)

    each_chunk(queries_for_peer)
    pl.semaphore_wait(barrier, 3 + jnp.where(z > 0, 1, 0) + jnp.where(z < last, 1, 0))
    sends = exchange(True)
    arrivals = exchange(False)
    sends[0].start()
    each_chunk(queries_own)
    arrivals[0].wait_recv()

    def launch(chunk):
        pl.when(z < last)(lambda: query_copy(True, z, chunk).start())
        pl.when(z > 0)(lambda: query_copy(False, z, chunk).start())

    each_chunk(launch)
    each_chunk(kv_for_peer)
    for copy in sends[1:]:
        copy.start()
    each_chunk(kv_own)
    for copy in arrivals[1:]:
        copy.wait_recv()

    def turn_values(chunk):
        for i in range(PER):
            unit = chunk * PER + i
            vals_t[unit] = vals[unit].astype(F32).T.astype(BF16)

    each_chunk(turn_values)
    each_chunk(lambda chunk: attend(z, chunk))

    for step in range(1, CHIPS):
        def at_step(chunk, step=step):
            has_left = z >= step
            has_right = z + step <= last
            pl.when(has_left)(lambda: from_left(z - step, chunk))
            pl.when(has_right)(lambda: from_right(z + step, chunk))
            pl.when(has_left)(lambda: attend(z - step, chunk))
            pl.when(has_right)(lambda: attend(z + step, chunk))
            pl.when(step > z)(lambda: relay(True, step, chunk))
            pl.when(last - step < z)(lambda: relay(False, last - step, chunk))
            if step == last:
                pl.when(chunk > 0)(lambda: conclude(chunk - 1))

        each_chunk(at_step)

    w_copy.wait()
    project(0)
    conclude(CHUNKS - 1)
    for n in range(2):
        x_out[n] = layer(0, n)
        x_copy(n).start()
    project(1)

    moved = jnp.float32(0.0)
    for i, size in enumerate(step_sizes()):
        moved = jnp.where(sidx[0] == i, jnp.float32(size), moved)
    amount = guidance[g]
    for n in range(2):
        cols = pl.ds(n * half, half)
        own = layer(1, n).astype(F32)
        x_copy(n).wait_recv()
        got = x_in[n].astype(F32)
        cond = jnp.where(g == 0, own, got)
        uncond = jnp.where(g == 0, got, own)
        guided = uncond + amount * (cond - uncond)
        guided_o[0, :, cols] = guided.astype(BF16)
        next_o[0, :, cols] = (latent[0, :, cols].astype(F32) + moved * guided).astype(BF16)

    for copy in sends:
        copy.wait_send()

    def drain(chunk):
        for owner in range(CHIPS):
            pl.when((z >= owner) & (z < last))(lambda: query_copy(True, owner, chunk).wait_send())
            pl.when((z <= owner) & (z > 0))(lambda: query_copy(False, owner, chunk).wait_send())

            @pl.when(z != owner)
            def _():
                for copy in part_copies(True, owner, chunk):
                    copy.wait_send()

        attn_copy(chunk, True).wait_send()

    each_chunk(drain)
    for n in range(2):
        y_copy(0, n).wait_send()
        y_copy(1, n).wait_send()
        x_copy(n).wait_send()


def fused_shards(
    img_hidden, img_query, img_key, img_value, txt_key, txt_value, query_gain, key_gain, gate,
    proj_weight, proj_bias, guidance, text_len, step_index, latent,
):
    width = img_query.shape[3]
    vmem = pl.BlockSpec(memory_space=pltpu.VMEM)
    smem = pl.BlockSpec(memory_space=pltpu.SMEM)
    away = pl.BlockSpec(memory_space=pl.ANY)
    dma = pltpu.SemaphoreType.DMA
    out = jax.ShapeDtypeStruct(latent.shape, BF16)
    block = (UNITS, 2 * ROWS, HD)
    return pl.pallas_call(
        fused,
        out_shape=(out, out),
        in_specs=[vmem] * 9 + [away, vmem, smem, smem, smem, vmem, away, vmem],
        out_specs=(vmem, vmem),
        scratch_shapes=[
            pltpu.VMEM(proj_weight.shape, BF16),
            pltpu.VMEM((ROWS, 2 * HD), F32),
            pltpu.VMEM((CHIPS,) + block, BF16),
            pltpu.VMEM((UNITS, 4 * ROWS, HD), BF16),
            pltpu.VMEM((UNITS, 4 * ROWS, HD), BF16),
            pltpu.VMEM((UNITS, HD, 4 * ROWS), BF16),
            pltpu.VMEM((UNITS, ROWS, HD), BF16),
            pltpu.VMEM((4, UNITS, ROWS, HD), BF16),
            pltpu.VMEM((CHIPS,) + block, F32),
            pltpu.VMEM((CHIPS, CHUNKS, 8, HD), F32),
            pltpu.VMEM((2, CHIPS) + block, BF16),
            pltpu.VMEM((2, CHIPS, CHUNKS, 8, HD), F32),
            pltpu.VMEM((CHIPS,) + block, BF16),
            pltpu.VMEM((CHIPS, CHUNKS, 8, HD), F32),
            pltpu.VMEM(block, BF16),
            pltpu.VMEM((2, 2 * HEADS_CORE, ROWS, HD), BF16),
            pltpu.VMEM((2, 2, ROWS, width // 2), BF16),
            pltpu.VMEM((2, 2, ROWS, width // 2), BF16),
            pltpu.VMEM((2, ROWS, width), F32),
            pltpu.VMEM((2, ROWS, width // 2), BF16),
            pltpu.VMEM((2, ROWS, width // 2), BF16),
            dma, dma,
            dma((5,)), dma((5,)),
            dma((2, CHIPS, CHUNKS)), dma((CHIPS, CHUNKS)),
            dma((CHIPS, CHUNKS)), dma((2, CHIPS, CHUNKS)),
            dma((CHIPS, CHUNKS)), dma((2, CHIPS, CHUNKS)),
            dma((CHUNKS,)), dma((CHUNKS,)),
            dma((2, 2)), dma((2, 2)),
            dma((2,)), dma((2,)),
        ],
        compiler_params=pltpu.CompilerParams(
            collective_id=0, has_side_effects=True, vmem_limit_bytes=52 * 2**20
        ),
        name="fused_step",
    )(
        img_hidden, img_query, img_key, img_value, txt_key, txt_value,
        query_gain.reshape(1, HD), key_gain, gate, proj_weight, proj_bias.reshape(1, width),
        guidance, text_len, step_index, latent,
        jnp.asarray(rope_table(2 * CHIPS)), jnp.asarray(swap_matrix(), BF16),
    )


def fits_fused(mesh):
    return mesh.shape["seq"] == 2 * CHIPS and mesh.shape["blk"] == 2 and mesh.shape["guide"] == 2


def solution(mesh):
    return jax.shard_map(
        fused_shards if fits_fused(mesh) else shards,
        mesh=mesh,
        in_specs=(
            P("guide", None, "seq", "blk"),
            P("guide", None, "seq", "blk"),
            P("guide", None, "seq", "blk"),
            P("guide", None, "seq", "blk"),
            P("guide", None, "seq", "blk"),
            P("guide", None, "seq", "blk"),
            P(),
            P(),
            P("guide", None, "blk"),
            P("blk", None),
            P("blk"),
            P(),
            P(),
            P(),
            P("guide", "seq", "blk"),
        ),
        out_specs=(P("guide", "seq", "blk"), P("guide", "seq", "blk")),
        check_vma=False,
    )
```

```python
import jax
import jax.numpy as jnp
import numpy as np
from jax import lax
from jax.experimental import pallas as pl
from jax.experimental.pallas import tpu as pltpu
from jax.sharding import PartitionSpec as P

HD = 128
GRID = 64
STEPS = 8


def rope_angles(positions):
    first = HD // 8
    second = (HD - first) // 2
    freqs = 10000.0 ** (-jnp.arange(0, second, 2).astype(jnp.float32) / second)
    rows = (positions // GRID).astype(jnp.float32)
    cols = (positions % GRID).astype(jnp.float32)
    zeros = jnp.zeros((positions.shape[0], first // 2), jnp.float32)
    return jnp.concatenate([zeros, rows[:, None] * freqs, cols[:, None] * freqs], -1)


def rotate(values, angles):
    pairs = values.reshape(values.shape[:-1] + (HD // 2, 2))
    cosine = jnp.cos(angles)[None, :, None, :]
    sine = jnp.sin(angles)[None, :, None, :]
    first = pairs[..., 0] * cosine - pairs[..., 1] * sine
    second = pairs[..., 0] * sine + pairs[..., 1] * cosine
    return jnp.stack([first, second], -1).reshape(values.shape)


def normed(values, gain_row):
    heads = values.astype(jnp.float32).reshape(
        values.shape[0], values.shape[1], values.shape[2] // HD, HD
    )
    return heads / jnp.sqrt(jnp.mean(heads * heads, -1, keepdims=True) + 1e-06) * gain_row


def shards(
    img_hidden,
    img_query,
    img_key,
    img_value,
    txt_key,
    txt_value,
    query_gain,
    key_gain,
    gate,
    proj_weight,
    proj_bias,
    guidance,
    text_len,
    step_index,
    latent,
):
    prompts = img_query.shape[1]
    img_here = img_query.shape[2]
    txt_here = txt_key.shape[2]
    width_here = img_query.shape[3]
    heads_here = width_here // HD
    slot_here = img_here + txt_here
    positions = lax.axis_index("seq") * img_here + jnp.arange(img_here)
    angles = rope_angles(positions)
    queries = rotate(normed(img_query[0], query_gain), angles).astype(jnp.bfloat16)
    keys_img = rotate(normed(img_key[0], key_gain[0]), angles).astype(jnp.bfloat16)
    keys_txt = normed(txt_key[0], key_gain[1]).astype(jnp.bfloat16)
    keys_local = jnp.concatenate([keys_txt, keys_img], 1).reshape(prompts, slot_here, width_here)
    values_local = jnp.concatenate([txt_value[0], img_value[0]], 1)
    running = jnp.full((prompts, img_here, heads_here), -1e30, jnp.float32)
    key_piece = lax.all_gather(keys_local, "seq", axis=1, tiled=True)
    value_piece = lax.all_gather(values_local, "seq", axis=1, tiled=True)
    count = key_piece.shape[1]
    index = jnp.arange(count)
    device = index // slot_here
    within = index % slot_here
    text_pos = device * txt_here + within
    live = (within >= txt_here)[None, :] | (text_pos[None, :] < text_len[:, None])
    key_heads = key_piece.reshape(prompts, count, heads_here, HD)
    value_heads = value_piece.reshape(prompts, count, heads_here, HD)
    scores = jnp.einsum(
        "pqhd,pkhd->pqhk", queries, key_heads, preferred_element_type=jnp.float32
    ) * HD ** (-0.5)
    mask = live[:, None, None, :]
    scores = jnp.where(mask, scores, -1e30)
    newest = jnp.maximum(running, jnp.max(scores, -1))
    expo = jnp.where(mask, jnp.exp(scores - newest[..., None]), 0.0)
    total = jnp.sum(expo, -1)
    accum = jnp.einsum(
        "pqhk,pkhd->pqhd",
        expo.astype(jnp.bfloat16),
        value_heads,
        preferred_element_type=jnp.float32,
    )
    running, total, accum = (newest, total, accum)
    attn = (accum / total[..., None]).astype(jnp.bfloat16).reshape(prompts * img_here, width_here)
    partial_value = jnp.dot(attn, proj_weight, preferred_element_type=jnp.float32)
    proj = lax.psum_scatter(
        partial_value.astype(jnp.bfloat16), "blk", scatter_dimension=1, tiled=True
    ).astype(jnp.float32)
    proj = (proj + proj_bias).reshape(prompts, img_here, width_here)
    layer_out = (img_hidden[0].astype(jnp.float32) + gate[0][:, None, :] * proj).astype(
        jnp.bfloat16
    )
    both_halves = lax.all_to_all(layer_out[None], "guide", split_axis=1, concat_axis=0, tiled=True)
    cond = both_halves[0].astype(jnp.float32)
    uncond = both_halves[1].astype(jnp.float32)
    own_prompts = cond.shape[0]
    scale_here = lax.dynamic_slice_in_dim(
        guidance, lax.axis_index("guide") * own_prompts, own_prompts, 0
    )
    guided_f = uncond + scale_here[:, None, None] * (cond - uncond)
    index = step_index[0]
    u_now = 1.0 - index.astype(jnp.float32) / STEPS
    u_next = 1.0 - (index + 1).astype(jnp.float32) / STEPS
    step_size = 3.0 * u_next / (1.0 + 2.0 * u_next) - 3.0 * u_now / (1.0 + 2.0 * u_now)
    next_state = (latent.astype(jnp.float32) + step_size * guided_f).astype(jnp.bfloat16)
    return (guided_f.astype(jnp.bfloat16), next_state)


CHIPS = 4
ROWS = 64
CHUNKS = 4
PER = 3
UNITS = CHUNKS * PER
HEADS_CORE = 6
SCALE = HD ** (-0.5)
SCALE2 = SCALE * float(np.log2(np.e))
F32 = jnp.float32
BF16 = jnp.bfloat16


def rope_table(devices):
    first = HD // 8
    second = (HD - first) // 2
    freqs = (10000.0 ** (-np.arange(0, second, 2).astype(np.float32) / second)).astype(np.float32)
    positions = np.arange(devices * ROWS)
    rows = (positions // GRID).astype(np.float32)[:, None] * freqs
    cols = (positions % GRID).astype(np.float32)[:, None] * freqs
    angles = np.concatenate([np.zeros((positions.size, first // 2), np.float32), rows, cols], -1)
    angles = np.repeat(angles, 2, -1)
    table = np.concatenate([np.cos(angles), np.sin(angles)], -1).astype(np.float32)
    return table.reshape(devices, ROWS, 2 * HD)


def swap_matrix():
    out = np.zeros((HD, HD), np.float32)
    for pair in range(HD // 2):
        out[2 * pair + 1, 2 * pair] = -1.0
        out[2 * pair, 2 * pair + 1] = 1.0
    return out


def step_sizes():
    def sigma(i):
        u = 1.0 - i / STEPS
        return 3.0 * u / (1.0 + 2.0 * u)

    return [sigma(i + 1) - sigma(i) for i in range(STEPS)]


def fused(
    hid_hbm, q_hbm, ki_hbm, vi_hbm, kt_hbm, vt_hbm, qg_hbm, kg_hbm, gate_hbm, w_hbm, bias_hbm,
    guidance, tlen, sidx, latent_hbm, rope_hbm, perm_hbm, guided_o, next_o,
    hid, q_in, ki_in, vi_in, kt_in, vt_in, qg, kg, gate, bias, latent, perm, load_sem,
    weight, rope, q_all, keys, vals, vals_t, stage_q, stage_kv, part, lse, in_part, in_lse,
    out_part, out_lse, own_t, attn, y_out, y_in, proj, x_out, x_in,
    w_sem, rope_sem, ex_send, ex_recv, q_send, q_recv, p_send, p_recv, s_send, s_recv,
    a_send, a_recv, y_send, y_recv, x_send, x_recv,
):
    g = lax.axis_index("guide")
    s = lax.axis_index("seq")
    b = lax.axis_index("blk")
    z = s // 2
    core = s % 2
    other = 1 - core
    peer = {"seq": 2 * z + other}
    left = {"seq": s - 2}
    right = {"seq": s + 2}
    y_peer = {"blk": 1 - b}
    x_peer = {"guide": 1 - g}
    width = weight.shape[0]
    half = width // 2
    last = CHIPS - 1

    def prompt_of(order):
        return (1 - g) * (1 - order) + g * order

    def remote(src, dst, send, recv, device):
        return pltpu.make_async_remote_copy(
            src_ref=src, dst_ref=dst, send_sem=send, recv_sem=recv,
            device_id=device, device_id_type=pl.DeviceIdType.MESH,
        )

    barrier = pltpu.get_barrier_semaphore()

    def greet(device):
        pl.semaphore_signal(barrier, inc=1, device_id=device, device_id_type=pl.DeviceIdType.MESH)

    greet(peer)
    greet(y_peer)
    greet(x_peer)
    pl.when(z > 0)(lambda: greet(left))
    pl.when(z < last)(lambda: greet(right))

    rope_copy = pltpu.make_async_copy(rope_hbm.at[s], rope, rope_sem)
    rope_copy.start()
    loads = [
        pltpu.make_async_copy(src, dst, load_sem.at[n])
        for n, (src, dst) in enumerate([
            (q_hbm, q_in), (qg_hbm, qg), (perm_hbm, perm),
            (kt_hbm, kt_in), (ki_hbm, ki_in), (kg_hbm, kg), (vt_hbm, vt_in), (vi_hbm, vi_in),
            (hid_hbm, hid), (gate_hbm, gate), (bias_hbm, bias), (latent_hbm, latent),
        ])
    ]
    for load in loads:
        load.start()
    w_copy = pltpu.make_async_copy(w_hbm, weight, w_sem)
    w_copy.start()
    rope_copy.wait()
    for load in loads[:3]:
        load.wait()

    lane = lax.broadcasted_iota(jnp.int32, (8, HD), 1)

    def swapped(row):
        wide = jnp.broadcast_to(row, (8, HD))
        return jnp.where(
            lane % 2 == 0, pltpu.roll(wide, HD - 1, 1), pltpu.roll(wide, 1, 1)
        )[0:1]

    def scaled(values):
        return lax.rsqrt(jnp.mean(values * values, -1, keepdims=True) + 1e-06)

    def roped(values, gain):
        wide = values.astype(F32)
        turned = jnp.dot(values, perm[...], preferred_element_type=F32)
        cosine = rope[:, :HD] * gain
        sine = rope[:, HD:] * swapped(gain)
        return (scaled(wide) * (wide * cosine + turned * sine)).astype(BF16)

    def plain(values, gain):
        wide = values.astype(F32)
        return (wide * scaled(wide) * gain).astype(BF16)

    def each_chunk(step):
        def run(chunk, carry):
            step(chunk)
            return carry

        lax.fori_loop(0, CHUNKS, run, 0)

    def place(chunk, i, owner):
        order = chunk // 2
        head = owner * HEADS_CORE + (chunk % 2) * PER + i
        return prompt_of(order), pl.ds(pl.multiple_of(head * HD, HD), HD)

    mine = pl.ds(pl.multiple_of(core * ROWS, ROWS), ROWS)
    mine_img = pl.ds(pl.multiple_of((2 + core) * ROWS, ROWS), ROWS)
    theirs = pl.ds(pl.multiple_of(other * ROWS, ROWS), ROWS)
    theirs_img = pl.ds(pl.multiple_of((2 + other) * ROWS, ROWS), ROWS)

    def queries_for_peer(chunk):
        for i in range(PER):
            p, cols = place(chunk, i, other)
            stage_q[chunk * PER + i] = roped(q_in[0, p, :, cols], qg[...])

    def queries_own(chunk):
        for i in range(PER):
            p, cols = place(chunk, i, core)
            q_all[z, chunk * PER + i, mine, :] = roped(q_in[0, p, :, cols], qg[...])

    def kv_for_peer(chunk):
        for i in range(PER):
            p, cols = place(chunk, i, other)
            unit = chunk * PER + i
            stage_kv[0, unit] = plain(kt_in[0, p, :, cols], kg[1:2])
            stage_kv[1, unit] = roped(ki_in[0, p, :, cols], kg[0:1])
            stage_kv[2, unit] = vt_in[0, p, :, cols]
            stage_kv[3, unit] = vi_in[0, p, :, cols]

    def kv_own(chunk):
        for i in range(PER):
            p, cols = place(chunk, i, core)
            unit = chunk * PER + i
            keys[unit, mine, :] = plain(kt_in[0, p, :, cols], kg[1:2])
            keys[unit, mine_img, :] = roped(ki_in[0, p, :, cols], kg[0:1])
            vals[unit, mine, :] = vt_in[0, p, :, cols]
            vals[unit, mine_img, :] = vi_in[0, p, :, cols]

    def exchange(sending):
        rows, rows_img = (mine, mine_img) if sending else (theirs, theirs_img)
        pairs = [
            (stage_q, q_all.at[z, :, rows, :]),
            (stage_kv.at[0], keys.at[:, rows, :]),
            (stage_kv.at[1], keys.at[:, rows_img, :]),
            (stage_kv.at[2], vals.at[:, rows, :]),
            (stage_kv.at[3], vals.at[:, rows_img, :]),
        ]
        return [
            remote(src, dst, ex_send.at[n], ex_recv.at[n], peer)
            for n, (src, dst) in enumerate(pairs)
        ]

    def some(chunk):
        return pl.ds(chunk * PER, PER)

    def query_copy(to_right, owner, chunk):
        block = q_all.at[owner, some(chunk)]
        way = 1 if to_right else 0
        return remote(
            block, block, q_send.at[way, owner, chunk], q_recv.at[owner, chunk],
            right if to_right else left,
        )

    def part_copies(to_right, owner, chunk):
        way = 0 if to_right else 1
        device = right if to_right else left
        return (
            remote(
                out_part.at[owner, some(chunk)], in_part.at[way, owner, some(chunk)],
                p_send.at[owner, chunk], p_recv.at[way, owner, chunk], device,
            ),
            remote(
                out_lse.at[owner, chunk], in_lse.at[way, owner, chunk],
                s_send.at[owner, chunk], s_recv.at[way, owner, chunk], device,
            ),
        )

    def attend(owner, chunk):
        live_text = tlen[prompt_of(chunk // 2)]
        row = lax.broadcasted_iota(jnp.int32, (2 * ROWS, HD), 0)
        live = row + z * (2 * ROWS) < live_text
        units = [chunk * PER + i for i in range(PER)]
        scores = [
            lax.dot_general(
                keys[unit], q_all[owner, unit], (((1,), (1,)), ((), ())),
                preferred_element_type=F32,
            )
            for unit in units
        ]
        scores = [
            jnp.concatenate([jnp.where(live, raw[: 2 * ROWS], -1e30), raw[2 * ROWS :]], 0)
            for raw in scores
        ]
        tops = [jnp.max(raw, 0, keepdims=True) for raw in scores]
        expos = [jnp.exp2((raw - top) * SCALE2) for raw, top in zip(scores, tops)]
        totals = [jnp.sum(expo, 0, keepdims=True) for expo in expos]
        outs = [
            jnp.dot(vals_t[unit], expo.astype(BF16), preferred_element_type=F32)
            for unit, expo in zip(units, expos)
        ]
        for i in range(PER):
            part[owner, units[i]] = outs[i] * (1.0 / totals[i])
            lse[owner, chunk, i : i + 1, :] = tops[i] * SCALE + jnp.log(totals[i])

    def absorb(way, owner, chunk):
        for copy in part_copies(way == 0, owner, chunk):
            copy.wait_recv()
        for i in range(PER):
            unit = chunk * PER + i
            here = lse[owner, chunk, i : i + 1, :]
            there = in_lse[way, owner, chunk, i : i + 1, :]
            top = jnp.maximum(here, there)
            w_here = jnp.exp(here - top)
            w_there = jnp.exp(there - top)
            total = w_here + w_there
            part[owner, unit] = part[owner, unit] * (w_here / total) + in_part[
                way, owner, unit
            ].astype(F32) * (w_there / total)
            lse[owner, chunk, i : i + 1, :] = top + jnp.log(total)

    def relay(to_right, owner, chunk):
        if to_right:
            pl.when(z > 0)(lambda: absorb(0, owner, chunk))
        else:
            pl.when(z < last)(lambda: absorb(1, owner, chunk))
        out_part[owner, some(chunk)] = part[owner, some(chunk)].astype(BF16)
        out_lse[owner, chunk] = lse[owner, chunk]
        for copy in part_copies(to_right, owner, chunk):
            copy.start()

    def from_left(owner, chunk):
        query_copy(True, owner, chunk).wait_recv()
        pl.when(z < last)(lambda: query_copy(True, owner, chunk).start())

    def from_right(owner, chunk):
        query_copy(False, owner, chunk).wait_recv()
        pl.when(z > 0)(lambda: query_copy(False, owner, chunk).start())

    def attn_copy(chunk, sending):
        first = (core if sending else other) * HEADS_CORE + (chunk % 2) * PER
        return remote(
            own_t.at[some(chunk), theirs, :], attn.at[chunk // 2, pl.ds(first, PER)],
            a_send.at[chunk], a_recv.at[chunk], peer,
        )

    def conclude(chunk):
        pl.when(z > 0)(lambda: absorb(0, z, chunk))
        pl.when(z < last)(lambda: absorb(1, z, chunk))
        for i in range(PER):
            own_t[chunk * PER + i] = part[z, chunk * PER + i].T.astype(BF16)
        attn_copy(chunk, True).start()
        attn[chunk // 2, pl.ds(core * HEADS_CORE + (chunk % 2) * PER, PER)] = own_t[
            some(chunk), mine, :
        ]

    tile = 256

    def product(order, column):
        rows = jnp.concatenate([attn[order, h] for h in range(2 * HEADS_CORE)], -1)
        return jnp.dot(
            rows, weight[:, pl.ds(pl.multiple_of(column, tile), tile)],
            preferred_element_type=F32,
        )

    def y_copy(order, n):
        return remote(
            y_out.at[order, n], y_in.at[order, n], y_send.at[order, n], y_recv.at[order, n], y_peer
        )

    def project(order):
        for chunk in (2 * order, 2 * order + 1):
            attn_copy(chunk, False).wait_recv()
        for n in range(2):
            def send_tile(at, carry, n=n):
                start = pl.multiple_of(at * tile, tile)
                y_out[order, n, :, pl.ds(start, tile)] = product(
                    order, (1 - b) * width + n * half + start
                ).astype(BF16)
                return carry

            lax.fori_loop(0, half // tile, send_tile, 0)
            y_copy(order, n).start()

        def own_tile(at, carry):
            start = pl.multiple_of(at * tile, tile)
            proj[order, :, pl.ds(start, tile)] = product(order, b * width + start)
            return carry

        lax.fori_loop(0, width // tile, own_tile, 0)

    def x_copy(n):
        return remote(x_out.at[n], x_in.at[n], x_send.at[n], x_recv.at[n], x_peer)

    def layer(order, n):
        y_copy(order, n).wait_recv()
        p = prompt_of(order)
        cols = pl.ds(n * half, half)
        summed = proj[order, :, cols] + y_in[order, n].astype(F32) + bias[:, cols]
        return (
            hid[0, p, :, cols].astype(F32) + gate[0, pl.ds(p, 1), cols] * summed
        ).astype(BF16)

    each_chunk(queries_for_peer)
    pl.semaphore_wait(barrier, 3 + jnp.where(z > 0, 1, 0) + jnp.where(z < last, 1, 0))
    sends = exchange(True)
    arrivals = exchange(False)
    sends[0].start()
    each_chunk(queries_own)
    arrivals[0].wait_recv()

    def launch(chunk):
        pl.when(z < last)(lambda: query_copy(True, z, chunk).start())
        pl.when(z > 0)(lambda: query_copy(False, z, chunk).start())

    each_chunk(launch)
    for load in loads[3:8]:
        load.wait()
    each_chunk(kv_for_peer)
    for copy in sends[1:]:
        copy.start()
    each_chunk(kv_own)
    for copy in arrivals[1:]:
        copy.wait_recv()

    def turn_values(chunk):
        for i in range(PER):
            unit = chunk * PER + i
            vals_t[unit] = vals[unit].astype(F32).T.astype(BF16)

    each_chunk(turn_values)
    at_end = (z == 0) | (z == last)

    for step in range(1, CHIPS):
        def at_step(chunk, step=step):
            has_left = z >= step
            has_right = z + step <= last
            pl.when(has_left)(lambda: from_left(z - step, chunk))
            pl.when(has_right)(lambda: from_right(z + step, chunk))
            pl.when(has_left)(lambda: attend(z - step, chunk))
            pl.when(has_right)(lambda: attend(z + step, chunk))
            pl.when(step > z)(lambda: relay(True, step, chunk))
            pl.when(last - step < z)(lambda: relay(False, last - step, chunk))
            if step == 1:
                pl.when(at_end)(lambda: attend(z, chunk))
            if step == last:
                pl.when(jnp.logical_not(at_end))(lambda: attend(z, chunk))
                pl.when(chunk > 0)(lambda: conclude(chunk - 1))

        each_chunk(at_step)

    for load in loads[8:]:
        load.wait()
    w_copy.wait()
    project(0)
    conclude(CHUNKS - 1)
    for n in range(2):
        x_out[n] = layer(0, n)
        x_copy(n).start()
    project(1)

    moved = jnp.float32(0.0)
    for i, size in enumerate(step_sizes()):
        moved = jnp.where(sidx[0] == i, jnp.float32(size), moved)
    amount = guidance[g]
    for n in range(2):
        cols = pl.ds(n * half, half)
        own = layer(1, n).astype(F32)
        x_copy(n).wait_recv()
        got = x_in[n].astype(F32)
        cond = jnp.where(g == 0, own, got)
        uncond = jnp.where(g == 0, got, own)
        guided = uncond + amount * (cond - uncond)
        guided_o[0, :, cols] = guided.astype(BF16)
        next_o[0, :, cols] = (latent[0, :, cols].astype(F32) + moved * guided).astype(BF16)

    for copy in sends:
        copy.wait_send()

    def drain(chunk):
        for owner in range(CHIPS):
            pl.when((z >= owner) & (z < last))(lambda: query_copy(True, owner, chunk).wait_send())
            pl.when((z <= owner) & (z > 0))(lambda: query_copy(False, owner, chunk).wait_send())

            @pl.when(z != owner)
            def _():
                for copy in part_copies(True, owner, chunk):
                    copy.wait_send()

        attn_copy(chunk, True).wait_send()

    each_chunk(drain)
    for n in range(2):
        y_copy(0, n).wait_send()
        y_copy(1, n).wait_send()
        x_copy(n).wait_send()


def fused_shards(
    img_hidden, img_query, img_key, img_value, txt_key, txt_value, query_gain, key_gain, gate,
    proj_weight, proj_bias, guidance, text_len, step_index, latent,
):
    width = img_query.shape[3]
    vmem = pl.BlockSpec(memory_space=pltpu.VMEM)
    smem = pl.BlockSpec(memory_space=pltpu.SMEM)
    away = pl.BlockSpec(memory_space=pltpu.HBM)
    dma = pltpu.SemaphoreType.DMA
    out = jax.ShapeDtypeStruct(latent.shape, BF16)
    block = (UNITS, 2 * ROWS, HD)
    return pl.pallas_call(
        fused,
        out_shape=(out, out),
        in_specs=[away] * 11 + [smem] * 3 + [away] * 3,
        out_specs=(vmem, vmem),
        scratch_shapes=[
            *[pltpu.VMEM(img_query.shape, BF16)] * 6,
            pltpu.VMEM((1, HD), F32),
            pltpu.VMEM((2, HD), F32),
            pltpu.VMEM(gate.shape, F32),
            pltpu.VMEM((1, width), F32),
            pltpu.VMEM(latent.shape, BF16),
            pltpu.VMEM((HD, HD), BF16),
            dma((12,)),
            pltpu.VMEM(proj_weight.shape, BF16),
            pltpu.VMEM((ROWS, 2 * HD), F32),
            pltpu.VMEM((CHIPS,) + block, BF16),
            pltpu.VMEM((UNITS, 4 * ROWS, HD), BF16),
            pltpu.VMEM((UNITS, 4 * ROWS, HD), BF16),
            pltpu.VMEM((UNITS, HD, 4 * ROWS), BF16),
            pltpu.VMEM((UNITS, ROWS, HD), BF16),
            pltpu.VMEM((4, UNITS, ROWS, HD), BF16),
            pltpu.VMEM((CHIPS,) + block, F32),
            pltpu.VMEM((CHIPS, CHUNKS, 8, HD), F32),
            pltpu.VMEM((2, CHIPS) + block, BF16),
            pltpu.VMEM((2, CHIPS, CHUNKS, 8, HD), F32),
            pltpu.VMEM((CHIPS,) + block, BF16),
            pltpu.VMEM((CHIPS, CHUNKS, 8, HD), F32),
            pltpu.VMEM(block, BF16),
            pltpu.VMEM((2, 2 * HEADS_CORE, ROWS, HD), BF16),
            pltpu.VMEM((2, 2, ROWS, width // 2), BF16),
            pltpu.VMEM((2, 2, ROWS, width // 2), BF16),
            pltpu.VMEM((2, ROWS, width), F32),
            pltpu.VMEM((2, ROWS, width // 2), BF16),
            pltpu.VMEM((2, ROWS, width // 2), BF16),
            dma, dma,
            dma((5,)), dma((5,)),
            dma((2, CHIPS, CHUNKS)), dma((CHIPS, CHUNKS)),
            dma((CHIPS, CHUNKS)), dma((2, CHIPS, CHUNKS)),
            dma((CHIPS, CHUNKS)), dma((2, CHIPS, CHUNKS)),
            dma((CHUNKS,)), dma((CHUNKS,)),
            dma((2, 2)), dma((2, 2)),
            dma((2,)), dma((2,)),
        ],
        compiler_params=pltpu.CompilerParams(
            collective_id=0, has_side_effects=True, vmem_limit_bytes=60 * 2**20
        ),
        name="fused_step",
    )(
        img_hidden, img_query, img_key, img_value, txt_key, txt_value,
        query_gain.reshape(1, HD), key_gain, gate, proj_weight, proj_bias.reshape(1, width),
        guidance, text_len, step_index, latent,
        jnp.asarray(rope_table(2 * CHIPS)), jnp.asarray(swap_matrix(), BF16),
    )


def fits_fused(mesh):
    return mesh.shape["seq"] == 2 * CHIPS and mesh.shape["blk"] == 2 and mesh.shape["guide"] == 2


def solution(mesh):
    return jax.shard_map(
        fused_shards if fits_fused(mesh) else shards,
        mesh=mesh,
        in_specs=(
            P("guide", None, "seq", "blk"),
            P("guide", None, "seq", "blk"),
            P("guide", None, "seq", "blk"),
            P("guide", None, "seq", "blk"),
            P("guide", None, "seq", "blk"),
            P("guide", None, "seq", "blk"),
            P(),
            P(),
            P("guide", None, "blk"),
            P("blk", None),
            P("blk"),
            P(),
            P(),
            P(),
            P("guide", "seq", "blk"),
        ),
        out_specs=(P("guide", "seq", "blk"), P("guide", "seq", "blk")),
        check_vma=False,
    )
```

```python
import jax
import jax.numpy as jnp
import numpy as np
from jax import lax
from jax.experimental import pallas as pl
from jax.experimental.pallas import tpu as pltpu
from jax.sharding import PartitionSpec as P

HD = 128
GRID = 64
STEPS = 8


def rope_angles(positions):
    first = HD // 8
    second = (HD - first) // 2
    freqs = 10000.0 ** (-jnp.arange(0, second, 2).astype(jnp.float32) / second)
    rows = (positions // GRID).astype(jnp.float32)
    cols = (positions % GRID).astype(jnp.float32)
    zeros = jnp.zeros((positions.shape[0], first // 2), jnp.float32)
    return jnp.concatenate([zeros, rows[:, None] * freqs, cols[:, None] * freqs], -1)


def rotate(values, angles):
    pairs = values.reshape(values.shape[:-1] + (HD // 2, 2))
    cosine = jnp.cos(angles)[None, :, None, :]
    sine = jnp.sin(angles)[None, :, None, :]
    first = pairs[..., 0] * cosine - pairs[..., 1] * sine
    second = pairs[..., 0] * sine + pairs[..., 1] * cosine
    return jnp.stack([first, second], -1).reshape(values.shape)


def normed(values, gain_row):
    heads = values.astype(jnp.float32).reshape(
        values.shape[0], values.shape[1], values.shape[2] // HD, HD
    )
    return heads / jnp.sqrt(jnp.mean(heads * heads, -1, keepdims=True) + 1e-06) * gain_row


def shards(
    img_hidden,
    img_query,
    img_key,
    img_value,
    txt_key,
    txt_value,
    query_gain,
    key_gain,
    gate,
    proj_weight,
    proj_bias,
    guidance,
    text_len,
    step_index,
    latent,
):
    prompts = img_query.shape[1]
    img_here = img_query.shape[2]
    txt_here = txt_key.shape[2]
    width_here = img_query.shape[3]
    heads_here = width_here // HD
    slot_here = img_here + txt_here
    positions = lax.axis_index("seq") * img_here + jnp.arange(img_here)
    angles = rope_angles(positions)
    queries = rotate(normed(img_query[0], query_gain), angles).astype(jnp.bfloat16)
    keys_img = rotate(normed(img_key[0], key_gain[0]), angles).astype(jnp.bfloat16)
    keys_txt = normed(txt_key[0], key_gain[1]).astype(jnp.bfloat16)
    keys_local = jnp.concatenate([keys_txt, keys_img], 1).reshape(prompts, slot_here, width_here)
    values_local = jnp.concatenate([txt_value[0], img_value[0]], 1)
    running = jnp.full((prompts, img_here, heads_here), -1e30, jnp.float32)
    key_piece = lax.all_gather(keys_local, "seq", axis=1, tiled=True)
    value_piece = lax.all_gather(values_local, "seq", axis=1, tiled=True)
    count = key_piece.shape[1]
    index = jnp.arange(count)
    device = index // slot_here
    within = index % slot_here
    text_pos = device * txt_here + within
    live = (within >= txt_here)[None, :] | (text_pos[None, :] < text_len[:, None])
    key_heads = key_piece.reshape(prompts, count, heads_here, HD)
    value_heads = value_piece.reshape(prompts, count, heads_here, HD)
    scores = jnp.einsum(
        "pqhd,pkhd->pqhk", queries, key_heads, preferred_element_type=jnp.float32
    ) * HD ** (-0.5)
    mask = live[:, None, None, :]
    scores = jnp.where(mask, scores, -1e30)
    newest = jnp.maximum(running, jnp.max(scores, -1))
    expo = jnp.where(mask, jnp.exp(scores - newest[..., None]), 0.0)
    total = jnp.sum(expo, -1)
    accum = jnp.einsum(
        "pqhk,pkhd->pqhd",
        expo.astype(jnp.bfloat16),
        value_heads,
        preferred_element_type=jnp.float32,
    )
    running, total, accum = (newest, total, accum)
    attn = (accum / total[..., None]).astype(jnp.bfloat16).reshape(prompts * img_here, width_here)
    partial_value = jnp.dot(attn, proj_weight, preferred_element_type=jnp.float32)
    proj = lax.psum_scatter(
        partial_value.astype(jnp.bfloat16), "blk", scatter_dimension=1, tiled=True
    ).astype(jnp.float32)
    proj = (proj + proj_bias).reshape(prompts, img_here, width_here)
    layer_out = (img_hidden[0].astype(jnp.float32) + gate[0][:, None, :] * proj).astype(
        jnp.bfloat16
    )
    both_halves = lax.all_to_all(layer_out[None], "guide", split_axis=1, concat_axis=0, tiled=True)
    cond = both_halves[0].astype(jnp.float32)
    uncond = both_halves[1].astype(jnp.float32)
    own_prompts = cond.shape[0]
    scale_here = lax.dynamic_slice_in_dim(
        guidance, lax.axis_index("guide") * own_prompts, own_prompts, 0
    )
    guided_f = uncond + scale_here[:, None, None] * (cond - uncond)
    index = step_index[0]
    u_now = 1.0 - index.astype(jnp.float32) / STEPS
    u_next = 1.0 - (index + 1).astype(jnp.float32) / STEPS
    step_size = 3.0 * u_next / (1.0 + 2.0 * u_next) - 3.0 * u_now / (1.0 + 2.0 * u_now)
    next_state = (latent.astype(jnp.float32) + step_size * guided_f).astype(jnp.bfloat16)
    return (guided_f.astype(jnp.bfloat16), next_state)


CHIPS = 4
ROWS = 64
CHUNKS = 4
PER = 3
UNITS = CHUNKS * PER
HEADS_CORE = 6
SCALE = HD ** (-0.5)
SCALE2 = SCALE * float(np.log2(np.e))
F32 = jnp.float32
BF16 = jnp.bfloat16


def rope_table(devices):
    first = HD // 8
    second = (HD - first) // 2
    freqs = (10000.0 ** (-np.arange(0, second, 2).astype(np.float32) / second)).astype(np.float32)
    positions = np.arange(devices * ROWS)
    rows = (positions // GRID).astype(np.float32)[:, None] * freqs
    cols = (positions % GRID).astype(np.float32)[:, None] * freqs
    angles = np.concatenate([np.zeros((positions.size, first // 2), np.float32), rows, cols], -1)
    angles = np.repeat(angles, 2, -1)
    table = np.concatenate([np.cos(angles), np.sin(angles)], -1).astype(np.float32)
    return table.reshape(devices, ROWS, 2 * HD)


def swap_matrix():
    out = np.zeros((HD, HD), np.float32)
    for pair in range(HD // 2):
        out[2 * pair + 1, 2 * pair] = -1.0
        out[2 * pair, 2 * pair + 1] = 1.0
    return out


def fused(
    hid_hbm, q_hbm, ki_hbm, vi_hbm, kt_hbm, vt_hbm, qg_hbm, kg_hbm, gate_hbm, w_hbm, bias_hbm,
    guidance, tlen, rope_hbm, perm_hbm, guided_o,
    hid, q_in, ki_in, vi_in, kt_in, vt_in, qg, kg, gate, bias, perm, load_sem,
    weight, rope, q_all, keys, vals, vals_t, stage_q, stage_kv, part, lse, in_part, in_lse,
    out_part, out_lse, own_t, attn, y_out, y_in, proj, x_out, x_in,
    w_sem, rope_sem, ex_send, ex_recv, q_send, q_recv, p_send, p_recv, s_send, s_recv,
    a_send, a_recv, y_send, y_recv, x_send, x_recv,
):
    g = lax.axis_index("guide")
    s = lax.axis_index("seq")
    b = lax.axis_index("blk")
    z = s // 2
    core = s % 2
    other = 1 - core
    peer = {"seq": 2 * z + other}
    left = {"seq": s - 2}
    right = {"seq": s + 2}
    y_peer = {"blk": 1 - b}
    x_peer = {"guide": 1 - g}
    width = weight.shape[0]
    half = width // 2
    last = CHIPS - 1

    def prompt_of(order):
        return (1 - g) * (1 - order) + g * order

    def remote(src, dst, send, recv, device):
        return pltpu.make_async_remote_copy(
            src_ref=src, dst_ref=dst, send_sem=send, recv_sem=recv,
            device_id=device, device_id_type=pl.DeviceIdType.MESH,
        )

    barrier = pltpu.get_barrier_semaphore()

    def greet(device):
        pl.semaphore_signal(barrier, inc=1, device_id=device, device_id_type=pl.DeviceIdType.MESH)

    greet(peer)
    greet(y_peer)
    greet(x_peer)
    pl.when(z > 0)(lambda: greet(left))
    pl.when(z < last)(lambda: greet(right))

    rope_copy = pltpu.make_async_copy(rope_hbm.at[s], rope, rope_sem)
    rope_copy.start()
    loads = [
        pltpu.make_async_copy(src, dst, load_sem.at[n])
        for n, (src, dst) in enumerate([
            (q_hbm, q_in), (qg_hbm, qg), (perm_hbm, perm),
            (kt_hbm, kt_in), (ki_hbm, ki_in), (kg_hbm, kg), (vt_hbm, vt_in), (vi_hbm, vi_in),
            (hid_hbm, hid), (gate_hbm, gate), (bias_hbm, bias),
        ])
    ]
    for load in loads:
        load.start()
    w_copy = pltpu.make_async_copy(w_hbm, weight, w_sem)
    w_copy.start()
    rope_copy.wait()
    for load in loads[:3]:
        load.wait()

    lane = lax.broadcasted_iota(jnp.int32, (8, HD), 1)

    def swapped(row):
        wide = jnp.broadcast_to(row, (8, HD))
        return jnp.where(
            lane % 2 == 0, pltpu.roll(wide, HD - 1, 1), pltpu.roll(wide, 1, 1)
        )[0:1]

    def scaled(values):
        return lax.rsqrt(jnp.mean(values * values, -1, keepdims=True) + 1e-06)

    def roped(values, gain):
        wide = values.astype(F32)
        turned = jnp.dot(values, perm[...], preferred_element_type=F32)
        cosine = rope[:, :HD] * gain
        sine = rope[:, HD:] * swapped(gain)
        return (scaled(wide) * (wide * cosine + turned * sine)).astype(BF16)

    def plain(values, gain):
        wide = values.astype(F32)
        return (wide * scaled(wide) * gain).astype(BF16)

    def each_chunk(step):
        def run(chunk, carry):
            step(chunk)
            return carry

        lax.fori_loop(0, CHUNKS, run, 0)

    def place(chunk, i, owner):
        order = chunk // 2
        head = owner * HEADS_CORE + (chunk % 2) * PER + i
        return prompt_of(order), pl.ds(pl.multiple_of(head * HD, HD), HD)

    mine = pl.ds(pl.multiple_of(core * ROWS, ROWS), ROWS)
    mine_img = pl.ds(pl.multiple_of((2 + core) * ROWS, ROWS), ROWS)
    theirs = pl.ds(pl.multiple_of(other * ROWS, ROWS), ROWS)
    theirs_img = pl.ds(pl.multiple_of((2 + other) * ROWS, ROWS), ROWS)

    def queries_for_peer(chunk):
        for i in range(PER):
            p, cols = place(chunk, i, other)
            stage_q[chunk * PER + i] = roped(q_in[0, p, :, cols], qg[...])

    def queries_own(chunk):
        for i in range(PER):
            p, cols = place(chunk, i, core)
            q_all[z, chunk * PER + i, mine, :] = roped(q_in[0, p, :, cols], qg[...])

    def kv_for_peer(chunk):
        for i in range(PER):
            p, cols = place(chunk, i, other)
            unit = chunk * PER + i
            stage_kv[0, unit] = plain(kt_in[0, p, :, cols], kg[1:2])
            stage_kv[1, unit] = roped(ki_in[0, p, :, cols], kg[0:1])
            stage_kv[2, unit] = vt_in[0, p, :, cols]
            stage_kv[3, unit] = vi_in[0, p, :, cols]

    def kv_own(chunk):
        for i in range(PER):
            p, cols = place(chunk, i, core)
            unit = chunk * PER + i
            keys[unit, mine, :] = plain(kt_in[0, p, :, cols], kg[1:2])
            keys[unit, mine_img, :] = roped(ki_in[0, p, :, cols], kg[0:1])
            vals[unit, mine, :] = vt_in[0, p, :, cols]
            vals[unit, mine_img, :] = vi_in[0, p, :, cols]

    def exchange(sending):
        rows, rows_img = (mine, mine_img) if sending else (theirs, theirs_img)
        pairs = [
            (stage_q, q_all.at[z, :, rows, :]),
            (stage_kv.at[0], keys.at[:, rows, :]),
            (stage_kv.at[1], keys.at[:, rows_img, :]),
            (stage_kv.at[2], vals.at[:, rows, :]),
            (stage_kv.at[3], vals.at[:, rows_img, :]),
        ]
        return [
            remote(src, dst, ex_send.at[n], ex_recv.at[n], peer)
            for n, (src, dst) in enumerate(pairs)
        ]

    def some(chunk):
        return pl.ds(chunk * PER, PER)

    def query_copy(to_right, owner, chunk):
        block = q_all.at[owner, some(chunk)]
        way = 1 if to_right else 0
        return remote(
            block, block, q_send.at[way, owner, chunk], q_recv.at[owner, chunk],
            right if to_right else left,
        )

    def part_copies(to_right, owner, chunk):
        way = 0 if to_right else 1
        device = right if to_right else left
        return (
            remote(
                out_part.at[owner, some(chunk)], in_part.at[way, owner, some(chunk)],
                p_send.at[owner, chunk], p_recv.at[way, owner, chunk], device,
            ),
            remote(
                out_lse.at[owner, chunk], in_lse.at[way, owner, chunk],
                s_send.at[owner, chunk], s_recv.at[way, owner, chunk], device,
            ),
        )

    def attend(owner, chunk):
        live_text = tlen[prompt_of(chunk // 2)]
        row = lax.broadcasted_iota(jnp.int32, (2 * ROWS, HD), 0)
        live = row + z * (2 * ROWS) < live_text
        units = [chunk * PER + i for i in range(PER)]
        scores = [
            lax.dot_general(
                keys[unit], q_all[owner, unit], (((1,), (1,)), ((), ())),
                preferred_element_type=F32,
            )
            for unit in units
        ]
        scores = [
            jnp.concatenate([jnp.where(live, raw[: 2 * ROWS], -1e30), raw[2 * ROWS :]], 0)
            for raw in scores
        ]
        tops = [jnp.max(raw, 0, keepdims=True) for raw in scores]
        expos = [jnp.exp2((raw - top) * SCALE2) for raw, top in zip(scores, tops)]
        totals = [jnp.sum(expo, 0, keepdims=True) for expo in expos]
        outs = [
            jnp.dot(vals_t[unit], expo.astype(BF16), preferred_element_type=F32)
            for unit, expo in zip(units, expos)
        ]
        for i in range(PER):
            part[owner, units[i]] = outs[i] * (1.0 / totals[i])
            lse[owner, chunk, i : i + 1, :] = tops[i] * SCALE + jnp.log(totals[i])

    def absorb(way, owner, chunk):
        for copy in part_copies(way == 0, owner, chunk):
            copy.wait_recv()
        for i in range(PER):
            unit = chunk * PER + i
            here = lse[owner, chunk, i : i + 1, :]
            there = in_lse[way, owner, chunk, i : i + 1, :]
            top = jnp.maximum(here, there)
            w_here = jnp.exp(here - top)
            w_there = jnp.exp(there - top)
            total = w_here + w_there
            part[owner, unit] = part[owner, unit] * (w_here / total) + in_part[
                way, owner, unit
            ].astype(F32) * (w_there / total)
            lse[owner, chunk, i : i + 1, :] = top + jnp.log(total)

    def relay(to_right, owner, chunk):
        if to_right:
            pl.when(z > 0)(lambda: absorb(0, owner, chunk))
        else:
            pl.when(z < last)(lambda: absorb(1, owner, chunk))
        out_part[owner, some(chunk)] = part[owner, some(chunk)].astype(BF16)
        out_lse[owner, chunk] = lse[owner, chunk]
        for copy in part_copies(to_right, owner, chunk):
            copy.start()

    def from_left(owner, chunk):
        query_copy(True, owner, chunk).wait_recv()
        pl.when(z < last)(lambda: query_copy(True, owner, chunk).start())

    def from_right(owner, chunk):
        query_copy(False, owner, chunk).wait_recv()
        pl.when(z > 0)(lambda: query_copy(False, owner, chunk).start())

    def attn_copy(chunk, sending):
        first = (core if sending else other) * HEADS_CORE + (chunk % 2) * PER
        return remote(
            own_t.at[some(chunk), theirs, :], attn.at[chunk // 2, pl.ds(first, PER)],
            a_send.at[chunk], a_recv.at[chunk], peer,
        )

    def conclude(chunk):
        pl.when(z > 0)(lambda: absorb(0, z, chunk))
        pl.when(z < last)(lambda: absorb(1, z, chunk))
        for i in range(PER):
            own_t[chunk * PER + i] = part[z, chunk * PER + i].T.astype(BF16)
        attn_copy(chunk, True).start()
        attn[chunk // 2, pl.ds(core * HEADS_CORE + (chunk % 2) * PER, PER)] = own_t[
            some(chunk), mine, :
        ]

    tile = 256

    def product(order, column):
        rows = jnp.concatenate([attn[order, h] for h in range(2 * HEADS_CORE)], -1)
        return jnp.dot(
            rows, weight[:, pl.ds(pl.multiple_of(column, tile), tile)],
            preferred_element_type=F32,
        )

    def y_copy(order, n):
        return remote(
            y_out.at[order, n], y_in.at[order, n], y_send.at[order, n], y_recv.at[order, n], y_peer
        )

    def project(order):
        for chunk in (2 * order, 2 * order + 1):
            attn_copy(chunk, False).wait_recv()
        for n in range(2):
            def send_tile(at, carry, n=n):
                start = pl.multiple_of(at * tile, tile)
                y_out[order, n, :, pl.ds(start, tile)] = product(
                    order, (1 - b) * width + n * half + start
                ).astype(BF16)
                return carry

            lax.fori_loop(0, half // tile, send_tile, 0)
            y_copy(order, n).start()

        def own_tile(at, carry):
            start = pl.multiple_of(at * tile, tile)
            proj[order, :, pl.ds(start, tile)] = product(order, b * width + start)
            return carry

        lax.fori_loop(0, width // tile, own_tile, 0)

    def x_copy(n):
        return remote(x_out.at[n], x_in.at[n], x_send.at[n], x_recv.at[n], x_peer)

    def layer(order, n):
        y_copy(order, n).wait_recv()
        p = prompt_of(order)
        cols = pl.ds(n * half, half)
        summed = proj[order, :, cols] + y_in[order, n].astype(F32) + bias[:, cols]
        return (
            hid[0, p, :, cols].astype(F32) + gate[0, pl.ds(p, 1), cols] * summed
        ).astype(BF16)

    each_chunk(queries_for_peer)
    pl.semaphore_wait(barrier, 3 + jnp.where(z > 0, 1, 0) + jnp.where(z < last, 1, 0))
    sends = exchange(True)
    arrivals = exchange(False)
    sends[0].start()
    each_chunk(queries_own)
    arrivals[0].wait_recv()

    def launch(chunk):
        pl.when(z < last)(lambda: query_copy(True, z, chunk).start())
        pl.when(z > 0)(lambda: query_copy(False, z, chunk).start())

    each_chunk(launch)
    for load in loads[3:8]:
        load.wait()
    each_chunk(kv_for_peer)
    for copy in sends[1:]:
        copy.start()
    each_chunk(kv_own)

    def turn_values(chunk):
        for i in range(PER):
            unit = chunk * PER + i
            vals_t[unit] = vals[unit].astype(F32).T.astype(BF16)

    at_end = (z == 0) | (z == last)

    def forward(step, chunk):
        pl.when(z >= step)(lambda: from_left(z - step, chunk))
        pl.when(z + step <= last)(lambda: from_right(z + step, chunk))

    each_chunk(lambda chunk: forward(1, chunk))
    for copy in arrivals[1:]:
        copy.wait_recv()
    each_chunk(turn_values)

    for step in range(1, CHIPS):
        def at_step(chunk, step=step):
            has_left = z >= step
            has_right = z + step <= last
            pl.when(has_left)(lambda: attend(z - step, chunk))
            pl.when(has_right)(lambda: attend(z + step, chunk))
            pl.when(step > z)(lambda: relay(True, step, chunk))
            pl.when(last - step < z)(lambda: relay(False, last - step, chunk))
            if step < last:
                forward(step + 1, chunk)
            if step == 1:
                pl.when(at_end)(lambda: attend(z, chunk))
            if step == last:
                pl.when(jnp.logical_not(at_end))(lambda: attend(z, chunk))
                pl.when(chunk > 0)(lambda: conclude(chunk - 1))

        each_chunk(at_step)

    for load in loads[8:]:
        load.wait()
    w_copy.wait()
    project(0)
    conclude(CHUNKS - 1)
    for n in range(2):
        x_out[n] = layer(0, n)
        x_copy(n).start()
    project(1)

    amount = guidance[g]
    for n in range(2):
        cols = pl.ds(n * half, half)
        own = layer(1, n).astype(F32)
        x_copy(n).wait_recv()
        got = x_in[n].astype(F32)
        cond = jnp.where(g == 0, own, got)
        uncond = jnp.where(g == 0, got, own)
        guided_o[0, :, cols] = uncond + amount * (cond - uncond)

    for copy in sends:
        copy.wait_send()

    def drain(chunk):
        for owner in range(CHIPS):
            pl.when((z >= owner) & (z < last))(lambda: query_copy(True, owner, chunk).wait_send())
            pl.when((z <= owner) & (z > 0))(lambda: query_copy(False, owner, chunk).wait_send())

            @pl.when(z != owner)
            def _():
                for copy in part_copies(True, owner, chunk):
                    copy.wait_send()

        attn_copy(chunk, True).wait_send()

    each_chunk(drain)
    for n in range(2):
        y_copy(0, n).wait_send()
        y_copy(1, n).wait_send()
        x_copy(n).wait_send()


def fused_shards(
    img_hidden, img_query, img_key, img_value, txt_key, txt_value, query_gain, key_gain, gate,
    proj_weight, proj_bias, guidance, text_len, step_index, latent,
):
    width = img_query.shape[3]
    vmem = pl.BlockSpec(memory_space=pltpu.VMEM)
    smem = pl.BlockSpec(memory_space=pltpu.SMEM)
    away = pl.BlockSpec(memory_space=pltpu.HBM)
    dma = pltpu.SemaphoreType.DMA
    block = (UNITS, 2 * ROWS, HD)
    guided_f = pl.pallas_call(
        fused,
        out_shape=jax.ShapeDtypeStruct(latent.shape, F32),
        in_specs=[away] * 11 + [smem] * 2 + [away] * 2,
        out_specs=vmem,
        scratch_shapes=[
            *[pltpu.VMEM(img_query.shape, BF16)] * 6,
            pltpu.VMEM((1, HD), F32),
            pltpu.VMEM((2, HD), F32),
            pltpu.VMEM(gate.shape, F32),
            pltpu.VMEM((1, width), F32),
            pltpu.VMEM((HD, HD), BF16),
            dma((11,)),
            pltpu.VMEM(proj_weight.shape, BF16),
            pltpu.VMEM((ROWS, 2 * HD), F32),
            pltpu.VMEM((CHIPS,) + block, BF16),
            pltpu.VMEM((UNITS, 4 * ROWS, HD), BF16),
            pltpu.VMEM((UNITS, 4 * ROWS, HD), BF16),
            pltpu.VMEM((UNITS, HD, 4 * ROWS), BF16),
            pltpu.VMEM((UNITS, ROWS, HD), BF16),
            pltpu.VMEM((4, UNITS, ROWS, HD), BF16),
            pltpu.VMEM((CHIPS,) + block, F32),
            pltpu.VMEM((CHIPS, CHUNKS, 8, HD), F32),
            pltpu.VMEM((2, CHIPS) + block, BF16),
            pltpu.VMEM((2, CHIPS, CHUNKS, 8, HD), F32),
            pltpu.VMEM((CHIPS,) + block, BF16),
            pltpu.VMEM((CHIPS, CHUNKS, 8, HD), F32),
            pltpu.VMEM(block, BF16),
            pltpu.VMEM((2, 2 * HEADS_CORE, ROWS, HD), BF16),
            pltpu.VMEM((2, 2, ROWS, width // 2), BF16),
            pltpu.VMEM((2, 2, ROWS, width // 2), BF16),
            pltpu.VMEM((2, ROWS, width), F32),
            pltpu.VMEM((2, ROWS, width // 2), BF16),
            pltpu.VMEM((2, ROWS, width // 2), BF16),
            dma, dma,
            dma((5,)), dma((5,)),
            dma((2, CHIPS, CHUNKS)), dma((CHIPS, CHUNKS)),
            dma((CHIPS, CHUNKS)), dma((2, CHIPS, CHUNKS)),
            dma((CHIPS, CHUNKS)), dma((2, CHIPS, CHUNKS)),
            dma((CHUNKS,)), dma((CHUNKS,)),
            dma((2, 2)), dma((2, 2)),
            dma((2,)), dma((2,)),
        ],
        compiler_params=pltpu.CompilerParams(
            collective_id=0, has_side_effects=True, vmem_limit_bytes=60 * 2**20
        ),
        name="fused_step",
    )(
        img_hidden, img_query, img_key, img_value, txt_key, txt_value,
        query_gain.reshape(1, HD), key_gain, gate, proj_weight, proj_bias.reshape(1, width),
        guidance, text_len,
        jnp.asarray(rope_table(2 * CHIPS)), jnp.asarray(swap_matrix(), BF16),
    )
    index = step_index[0]
    u_now = 1.0 - index.astype(F32) / STEPS
    u_next = 1.0 - (index + 1).astype(F32) / STEPS
    step_size = 3.0 * u_next / (1.0 + 2.0 * u_next) - 3.0 * u_now / (1.0 + 2.0 * u_now)
    next_state = (latent.astype(F32) + step_size * guided_f).astype(BF16)
    return (guided_f.astype(BF16), next_state)


def fits_fused(mesh):
    return mesh.shape["seq"] == 2 * CHIPS and mesh.shape["blk"] == 2 and mesh.shape["guide"] == 2


def solution(mesh):
    return jax.shard_map(
        fused_shards if fits_fused(mesh) else shards,
        mesh=mesh,
        in_specs=(
            P("guide", None, "seq", "blk"),
            P("guide", None, "seq", "blk"),
            P("guide", None, "seq", "blk"),
            P("guide", None, "seq", "blk"),
            P("guide", None, "seq", "blk"),
            P("guide", None, "seq", "blk"),
            P(),
            P(),
            P("guide", None, "blk"),
            P("blk", None),
            P("blk"),
            P(),
            P(),
            P(),
            P("guide", "seq", "blk"),
        ),
        out_specs=(P("guide", "seq", "blk"), P("guide", "seq", "blk")),
        check_vma=False,
    )
```

```python
import jax
import jax.numpy as jnp
import numpy as np
from jax import lax
from jax.experimental import pallas as pl
from jax.experimental.pallas import tpu as pltpu
from jax.sharding import PartitionSpec as P

HD = 128
GRID = 64
STEPS = 8


def rope_angles(positions):
    first = HD // 8
    second = (HD - first) // 2
    freqs = 10000.0 ** (-jnp.arange(0, second, 2).astype(jnp.float32) / second)
    rows = (positions // GRID).astype(jnp.float32)
    cols = (positions % GRID).astype(jnp.float32)
    zeros = jnp.zeros((positions.shape[0], first // 2), jnp.float32)
    return jnp.concatenate([zeros, rows[:, None] * freqs, cols[:, None] * freqs], -1)


def rotate(values, angles):
    pairs = values.reshape(values.shape[:-1] + (HD // 2, 2))
    cosine = jnp.cos(angles)[None, :, None, :]
    sine = jnp.sin(angles)[None, :, None, :]
    first = pairs[..., 0] * cosine - pairs[..., 1] * sine
    second = pairs[..., 0] * sine + pairs[..., 1] * cosine
    return jnp.stack([first, second], -1).reshape(values.shape)


def normed(values, gain_row):
    heads = values.astype(jnp.float32).reshape(
        values.shape[0], values.shape[1], values.shape[2] // HD, HD
    )
    return heads / jnp.sqrt(jnp.mean(heads * heads, -1, keepdims=True) + 1e-06) * gain_row


def shards(
    img_hidden,
    img_query,
    img_key,
    img_value,
    txt_key,
    txt_value,
    query_gain,
    key_gain,
    gate,
    proj_weight,
    proj_bias,
    guidance,
    text_len,
    step_index,
    latent,
):
    prompts = img_query.shape[1]
    img_here = img_query.shape[2]
    txt_here = txt_key.shape[2]
    width_here = img_query.shape[3]
    heads_here = width_here // HD
    slot_here = img_here + txt_here
    positions = lax.axis_index("seq") * img_here + jnp.arange(img_here)
    angles = rope_angles(positions)
    queries = rotate(normed(img_query[0], query_gain), angles).astype(jnp.bfloat16)
    keys_img = rotate(normed(img_key[0], key_gain[0]), angles).astype(jnp.bfloat16)
    keys_txt = normed(txt_key[0], key_gain[1]).astype(jnp.bfloat16)
    keys_local = jnp.concatenate([keys_txt, keys_img], 1).reshape(prompts, slot_here, width_here)
    values_local = jnp.concatenate([txt_value[0], img_value[0]], 1)
    running = jnp.full((prompts, img_here, heads_here), -1e30, jnp.float32)
    key_piece = lax.all_gather(keys_local, "seq", axis=1, tiled=True)
    value_piece = lax.all_gather(values_local, "seq", axis=1, tiled=True)
    count = key_piece.shape[1]
    index = jnp.arange(count)
    device = index // slot_here
    within = index % slot_here
    text_pos = device * txt_here + within
    live = (within >= txt_here)[None, :] | (text_pos[None, :] < text_len[:, None])
    key_heads = key_piece.reshape(prompts, count, heads_here, HD)
    value_heads = value_piece.reshape(prompts, count, heads_here, HD)
    scores = jnp.einsum(
        "pqhd,pkhd->pqhk", queries, key_heads, preferred_element_type=jnp.float32
    ) * HD ** (-0.5)
    mask = live[:, None, None, :]
    scores = jnp.where(mask, scores, -1e30)
    newest = jnp.maximum(running, jnp.max(scores, -1))
    expo = jnp.where(mask, jnp.exp(scores - newest[..., None]), 0.0)
    total = jnp.sum(expo, -1)
    accum = jnp.einsum(
        "pqhk,pkhd->pqhd",
        expo.astype(jnp.bfloat16),
        value_heads,
        preferred_element_type=jnp.float32,
    )
    running, total, accum = (newest, total, accum)
    attn = (accum / total[..., None]).astype(jnp.bfloat16).reshape(prompts * img_here, width_here)
    partial_value = jnp.dot(attn, proj_weight, preferred_element_type=jnp.float32)
    proj = lax.psum_scatter(
        partial_value.astype(jnp.bfloat16), "blk", scatter_dimension=1, tiled=True
    ).astype(jnp.float32)
    proj = (proj + proj_bias).reshape(prompts, img_here, width_here)
    layer_out = (img_hidden[0].astype(jnp.float32) + gate[0][:, None, :] * proj).astype(
        jnp.bfloat16
    )
    both_halves = lax.all_to_all(layer_out[None], "guide", split_axis=1, concat_axis=0, tiled=True)
    cond = both_halves[0].astype(jnp.float32)
    uncond = both_halves[1].astype(jnp.float32)
    own_prompts = cond.shape[0]
    scale_here = lax.dynamic_slice_in_dim(
        guidance, lax.axis_index("guide") * own_prompts, own_prompts, 0
    )
    guided_f = uncond + scale_here[:, None, None] * (cond - uncond)
    index = step_index[0]
    u_now = 1.0 - index.astype(jnp.float32) / STEPS
    u_next = 1.0 - (index + 1).astype(jnp.float32) / STEPS
    step_size = 3.0 * u_next / (1.0 + 2.0 * u_next) - 3.0 * u_now / (1.0 + 2.0 * u_now)
    next_state = (latent.astype(jnp.float32) + step_size * guided_f).astype(jnp.bfloat16)
    return (guided_f.astype(jnp.bfloat16), next_state)


CHIPS = 4
ROWS = 64
CHUNKS = 4
PER = 3
UNITS = CHUNKS * PER
HEADS_CORE = 6
SCALE = HD ** (-0.5)
SCALE2 = SCALE * float(np.log2(np.e))
F32 = jnp.float32
BF16 = jnp.bfloat16


def rope_table(devices):
    first = HD // 8
    second = (HD - first) // 2
    freqs = (10000.0 ** (-np.arange(0, second, 2).astype(np.float32) / second)).astype(np.float32)
    positions = np.arange(devices * ROWS)
    rows = (positions // GRID).astype(np.float32)[:, None] * freqs
    cols = (positions % GRID).astype(np.float32)[:, None] * freqs
    angles = np.concatenate([np.zeros((positions.size, first // 2), np.float32), rows, cols], -1)
    angles = np.repeat(angles, 2, -1)
    table = np.concatenate([np.cos(angles), np.sin(angles)], -1).astype(np.float32)
    return table.reshape(devices, ROWS, 2 * HD)


def swap_matrix():
    out = np.zeros((HD, HD), np.float32)
    for pair in range(HD // 2):
        out[2 * pair + 1, 2 * pair] = -1.0
        out[2 * pair, 2 * pair + 1] = 1.0
    return out


def fused(
    hid_hbm, q_hbm, ki_hbm, vi_hbm, kt_hbm, vt_hbm, qg_hbm, kg_hbm, gate_hbm, w_hbm, bias_hbm,
    guidance, tlen, rope_hbm, perm_hbm, guided_o,
    hid, q_in, ki_in, vi_in, kt_in, vt_in, qg, kg, gate, bias, perm, load_sem,
    weight, rope, q_all, keys, vals, vals_t, stage_q, stage_kv, part, lse, in_part, in_lse,
    out_part, out_lse, own_t, attn, y_out, y_in, proj, x_out, x_in,
    w_sem, rope_sem, ex_send, ex_recv, q_send, q_recv, p_send, p_recv, s_send, s_recv,
    a_send, a_recv, y_send, y_recv, x_send, x_recv,
):
    g = lax.axis_index("guide")
    s = lax.axis_index("seq")
    b = lax.axis_index("blk")
    z = s // 2
    core = s % 2
    other = 1 - core
    peer = {"seq": 2 * z + other}
    left = {"seq": s - 2}
    right = {"seq": s + 2}
    y_peer = {"blk": 1 - b}
    x_peer = {"guide": 1 - g}
    width = weight.shape[0]
    half = width // 2
    last = CHIPS - 1

    def prompt_of(order):
        return (1 - g) * (1 - order) + g * order

    def remote(src, dst, send, recv, device):
        return pltpu.make_async_remote_copy(
            src_ref=src, dst_ref=dst, send_sem=send, recv_sem=recv,
            device_id=device, device_id_type=pl.DeviceIdType.MESH,
        )

    barrier = pltpu.get_barrier_semaphore()

    def greet(device):
        pl.semaphore_signal(barrier, inc=1, device_id=device, device_id_type=pl.DeviceIdType.MESH)

    greet(peer)
    greet(y_peer)
    greet(x_peer)
    pl.when(z > 0)(lambda: greet(left))
    pl.when(z < last)(lambda: greet(right))

    rope_copy = pltpu.make_async_copy(rope_hbm.at[s], rope, rope_sem)
    rope_copy.start()
    loads = [
        pltpu.make_async_copy(src, dst, load_sem.at[n])
        for n, (src, dst) in enumerate([
            (q_hbm, q_in), (qg_hbm, qg), (perm_hbm, perm),
            (kt_hbm, kt_in), (ki_hbm, ki_in), (kg_hbm, kg), (vt_hbm, vt_in), (vi_hbm, vi_in),
            (hid_hbm, hid), (gate_hbm, gate), (bias_hbm, bias),
        ])
    ]
    for load in loads:
        load.start()
    w_copy = pltpu.make_async_copy(w_hbm, weight, w_sem)
    w_copy.start()
    rope_copy.wait()
    for load in loads[:3]:
        load.wait()

    lane = lax.broadcasted_iota(jnp.int32, (8, HD), 1)

    def swapped(row):
        wide = jnp.broadcast_to(row, (8, HD))
        return jnp.where(
            lane % 2 == 0, pltpu.roll(wide, HD - 1, 1), pltpu.roll(wide, 1, 1)
        )[0:1]

    def scaled(values):
        return lax.rsqrt(jnp.mean(values * values, -1, keepdims=True) + 1e-06)

    def roped(values, gain):
        wide = values.astype(F32)
        turned = jnp.dot(values, perm[...], preferred_element_type=F32)
        cosine = rope[:, :HD] * gain
        sine = rope[:, HD:] * swapped(gain)
        return (scaled(wide) * (wide * cosine + turned * sine)).astype(BF16)

    def plain(values, gain):
        wide = values.astype(F32)
        return (wide * scaled(wide) * gain).astype(BF16)

    def each_chunk(step):
        def run(chunk, carry):
            step(chunk)
            return carry

        lax.fori_loop(0, CHUNKS, run, 0)

    def place(chunk, i, owner):
        order = chunk // 2
        head = owner * HEADS_CORE + (chunk % 2) * PER + i
        return prompt_of(order), pl.ds(pl.multiple_of(head * HD, HD), HD)

    mine = pl.ds(pl.multiple_of(core * ROWS, ROWS), ROWS)
    mine_img = pl.ds(pl.multiple_of((2 + core) * ROWS, ROWS), ROWS)
    theirs = pl.ds(pl.multiple_of(other * ROWS, ROWS), ROWS)
    theirs_img = pl.ds(pl.multiple_of((2 + other) * ROWS, ROWS), ROWS)

    def queries_for_peer(chunk):
        for i in range(PER):
            p, cols = place(chunk, i, other)
            stage_q[chunk * PER + i] = roped(q_in[0, p, :, cols], qg[...])

    def queries_own(chunk):
        for i in range(PER):
            p, cols = place(chunk, i, core)
            q_all[z, chunk * PER + i, mine, :] = roped(q_in[0, p, :, cols], qg[...])

    def kv_for_peer(chunk):
        for i in range(PER):
            p, cols = place(chunk, i, other)
            unit = chunk * PER + i
            stage_kv[0, unit] = plain(kt_in[0, p, :, cols], kg[1:2])
            stage_kv[1, unit] = roped(ki_in[0, p, :, cols], kg[0:1])
            stage_kv[2, unit] = vt_in[0, p, :, cols]
            stage_kv[3, unit] = vi_in[0, p, :, cols]

    def kv_own(chunk):
        for i in range(PER):
            p, cols = place(chunk, i, core)
            unit = chunk * PER + i
            keys[unit, mine, :] = plain(kt_in[0, p, :, cols], kg[1:2])
            keys[unit, mine_img, :] = roped(ki_in[0, p, :, cols], kg[0:1])
            vals[unit, mine, :] = vt_in[0, p, :, cols]
            vals[unit, mine_img, :] = vi_in[0, p, :, cols]

    def exchange(sending):
        rows, rows_img = (mine, mine_img) if sending else (theirs, theirs_img)
        pairs = [
            (stage_q, q_all.at[z, :, rows, :]),
            (stage_kv.at[0], keys.at[:, rows, :]),
            (stage_kv.at[1], keys.at[:, rows_img, :]),
            (stage_kv.at[2], vals.at[:, rows, :]),
            (stage_kv.at[3], vals.at[:, rows_img, :]),
        ]
        return [
            remote(src, dst, ex_send.at[n], ex_recv.at[n], peer)
            for n, (src, dst) in enumerate(pairs)
        ]

    def some(chunk):
        return pl.ds(chunk * PER, PER)

    def query_copy(to_right, owner, chunk):
        block = q_all.at[owner, some(chunk)]
        way = 1 if to_right else 0
        return remote(
            block, block, q_send.at[way, owner, chunk], q_recv.at[owner, chunk],
            right if to_right else left,
        )

    def part_copies(to_right, owner, chunk):
        way = 0 if to_right else 1
        device = right if to_right else left
        return (
            remote(
                out_part.at[owner, some(chunk)], in_part.at[way, owner, some(chunk)],
                p_send.at[owner, chunk], p_recv.at[way, owner, chunk], device,
            ),
            remote(
                out_lse.at[owner, chunk], in_lse.at[way, owner, chunk],
                s_send.at[owner, chunk], s_recv.at[way, owner, chunk], device,
            ),
        )

    def attend(owner, chunk):
        live_text = tlen[prompt_of(chunk // 2)]
        row = lax.broadcasted_iota(jnp.int32, (2 * ROWS, HD), 0)
        live = row + z * (2 * ROWS) < live_text
        units = [chunk * PER + i for i in range(PER)]
        scores = [
            lax.dot_general(
                keys[unit], q_all[owner, unit], (((1,), (1,)), ((), ())),
                preferred_element_type=F32,
            )
            for unit in units
        ]
        scores = [
            jnp.concatenate([jnp.where(live, raw[: 2 * ROWS], -1e30), raw[2 * ROWS :]], 0)
            for raw in scores
        ]
        tops = [jnp.max(raw, 0, keepdims=True) for raw in scores]
        expos = [jnp.exp2((raw - top) * SCALE2) for raw, top in zip(scores, tops)]
        totals = [jnp.sum(expo, 0, keepdims=True) for expo in expos]
        outs = [
            jnp.dot(vals_t[unit], expo.astype(BF16), preferred_element_type=F32)
            for unit, expo in zip(units, expos)
        ]
        for i in range(PER):
            part[owner, units[i]] = outs[i] * (1.0 / totals[i])
            lse[owner, chunk, i : i + 1, :] = tops[i] * SCALE + jnp.log(totals[i])

    def absorb(way, owner, chunk):
        for copy in part_copies(way == 0, owner, chunk):
            copy.wait_recv()
        for i in range(PER):
            unit = chunk * PER + i
            here = lse[owner, chunk, i : i + 1, :]
            there = in_lse[way, owner, chunk, i : i + 1, :]
            top = jnp.maximum(here, there)
            w_here = jnp.exp(here - top)
            w_there = jnp.exp(there - top)
            total = w_here + w_there
            part[owner, unit] = part[owner, unit] * (w_here / total) + in_part[
                way, owner, unit
            ].astype(F32) * (w_there / total)
            lse[owner, chunk, i : i + 1, :] = top + jnp.log(total)

    def relay(to_right, owner, chunk):
        if to_right:
            pl.when(z > 0)(lambda: absorb(0, owner, chunk))
        else:
            pl.when(z < last)(lambda: absorb(1, owner, chunk))
        out_part[owner, some(chunk)] = part[owner, some(chunk)].astype(BF16)
        out_lse[owner, chunk] = lse[owner, chunk]
        for copy in part_copies(to_right, owner, chunk):
            copy.start()

    def from_left(owner, chunk):
        query_copy(True, owner, chunk).wait_recv()
        pl.when(z < last)(lambda: query_copy(True, owner, chunk).start())

    def from_right(owner, chunk):
        query_copy(False, owner, chunk).wait_recv()
        pl.when(z > 0)(lambda: query_copy(False, owner, chunk).start())

    def attn_copy(chunk, sending):
        first = (core if sending else other) * HEADS_CORE + (chunk % 2) * PER
        return remote(
            own_t.at[some(chunk), theirs, :], attn.at[chunk // 2, pl.ds(first, PER)],
            a_send.at[chunk], a_recv.at[chunk], peer,
        )

    def conclude(chunk):
        pl.when(z > 0)(lambda: absorb(0, z, chunk))
        pl.when(z < last)(lambda: absorb(1, z, chunk))
        for i in range(PER):
            own_t[chunk * PER + i] = part[z, chunk * PER + i].T.astype(BF16)
        attn_copy(chunk, True).start()
        attn[chunk // 2, pl.ds(core * HEADS_CORE + (chunk % 2) * PER, PER)] = own_t[
            some(chunk), mine, :
        ]

    tile = 256

    def product(order, column):
        rows = jnp.concatenate([attn[order, h] for h in range(2 * HEADS_CORE)], -1)
        return jnp.dot(
            rows, weight[:, pl.ds(pl.multiple_of(column, tile), tile)],
            preferred_element_type=F32,
        )

    def y_copy(order, n):
        return remote(
            y_out.at[order, n], y_in.at[order, n], y_send.at[order, n], y_recv.at[order, n], y_peer
        )

    def project(order):
        for chunk in (2 * order, 2 * order + 1):
            attn_copy(chunk, False).wait_recv()
        for n in range(2):
            def send_tile(at, carry, n=n):
                start = pl.multiple_of(at * tile, tile)
                y_out[order, n, :, pl.ds(start, tile)] = product(
                    order, (1 - b) * width + n * half + start
                ).astype(BF16)
                return carry

            lax.fori_loop(0, half // tile, send_tile, 0)
            y_copy(order, n).start()

        def own_tile(at, carry):
            start = pl.multiple_of(at * tile, tile)
            proj[order, :, pl.ds(start, tile)] = product(order, b * width + start)
            return carry

        lax.fori_loop(0, width // tile, own_tile, 0)

    def x_copy(n):
        return remote(x_out.at[n], x_in.at[n], x_send.at[n], x_recv.at[n], x_peer)

    def layer(order, n):
        y_copy(order, n).wait_recv()
        p = prompt_of(order)
        cols = pl.ds(n * half, half)
        summed = proj[order, :, cols] + y_in[order, n].astype(F32) + bias[:, cols]
        return (
            hid[0, p, :, cols].astype(F32) + gate[0, pl.ds(p, 1), cols] * summed
        ).astype(BF16)

    each_chunk(queries_for_peer)
    pl.semaphore_wait(barrier, 3 + jnp.where(z > 0, 1, 0) + jnp.where(z < last, 1, 0))
    sends = exchange(True)
    arrivals = exchange(False)
    sends[0].start()
    each_chunk(queries_own)
    arrivals[0].wait_recv()

    def launch(chunk):
        pl.when(z < last)(lambda: query_copy(True, z, chunk).start())
        pl.when(z > 0)(lambda: query_copy(False, z, chunk).start())

    each_chunk(launch)
    for load in loads[3:8]:
        load.wait()
    each_chunk(kv_for_peer)
    for copy in sends[1:]:
        copy.start()
    each_chunk(kv_own)
    for copy in arrivals[1:]:
        copy.wait_recv()

    def turn_values(chunk):
        for i in range(PER):
            unit = chunk * PER + i
            vals_t[unit] = vals[unit].astype(F32).T.astype(BF16)

    each_chunk(turn_values)
    at_end = (z == 0) | (z == last)

    for step in range(1, CHIPS):
        def at_step(chunk, step=step):
            has_left = z >= step
            has_right = z + step <= last
            pl.when(has_left)(lambda: from_left(z - step, chunk))
            pl.when(has_right)(lambda: from_right(z + step, chunk))
            pl.when(has_left)(lambda: attend(z - step, chunk))
            pl.when(has_right)(lambda: attend(z + step, chunk))
            pl.when(step > z)(lambda: relay(True, step, chunk))
            pl.when(last - step < z)(lambda: relay(False, last - step, chunk))
            if step == 1:
                pl.when(at_end)(lambda: attend(z, chunk))
            if step == last:
                pl.when(jnp.logical_not(at_end))(lambda: attend(z, chunk))
                pl.when(chunk > 0)(lambda: conclude(chunk - 1))

        each_chunk(at_step)

    for load in loads[8:]:
        load.wait()
    w_copy.wait()
    project(0)
    conclude(CHUNKS - 1)
    for n in range(2):
        x_out[n] = layer(0, n)
        x_copy(n).start()
    project(1)

    amount = guidance[g]
    for n in range(2):
        cols = pl.ds(n * half, half)
        own = layer(1, n).astype(F32)
        x_copy(n).wait_recv()
        got = x_in[n].astype(F32)
        cond = jnp.where(g == 0, own, got)
        uncond = jnp.where(g == 0, got, own)
        guided_o[0, :, cols] = uncond + amount * (cond - uncond)

    for copy in sends:
        copy.wait_send()

    def drain(chunk):
        for owner in range(CHIPS):
            pl.when((z >= owner) & (z < last))(lambda: query_copy(True, owner, chunk).wait_send())
            pl.when((z <= owner) & (z > 0))(lambda: query_copy(False, owner, chunk).wait_send())

            @pl.when(z != owner)
            def _():
                for copy in part_copies(True, owner, chunk):
                    copy.wait_send()

        attn_copy(chunk, True).wait_send()

    each_chunk(drain)
    for n in range(2):
        y_copy(0, n).wait_send()
        y_copy(1, n).wait_send()
        x_copy(n).wait_send()


def fused_shards(
    img_hidden, img_query, img_key, img_value, txt_key, txt_value, query_gain, key_gain, gate,
    proj_weight, proj_bias, guidance, text_len, step_index, latent,
):
    width = img_query.shape[3]
    vmem = pl.BlockSpec(memory_space=pltpu.VMEM)
    smem = pl.BlockSpec(memory_space=pltpu.SMEM)
    away = pl.BlockSpec(memory_space=pltpu.HBM)
    dma = pltpu.SemaphoreType.DMA
    block = (UNITS, 2 * ROWS, HD)
    guided_f = pl.pallas_call(
        fused,
        out_shape=jax.ShapeDtypeStruct(latent.shape, F32),
        in_specs=[away] * 11 + [smem] * 2 + [away] * 2,
        out_specs=vmem,
        scratch_shapes=[
            *[pltpu.VMEM(img_query.shape, BF16)] * 6,
            pltpu.VMEM((1, HD), F32),
            pltpu.VMEM((2, HD), F32),
            pltpu.VMEM(gate.shape, F32),
            pltpu.VMEM((1, width), F32),
            pltpu.VMEM((HD, HD), BF16),
            dma((11,)),
            pltpu.VMEM(proj_weight.shape, BF16),
            pltpu.VMEM((ROWS, 2 * HD), F32),
            pltpu.VMEM((CHIPS,) + block, BF16),
            pltpu.VMEM((UNITS, 4 * ROWS, HD), BF16),
            pltpu.VMEM((UNITS, 4 * ROWS, HD), BF16),
            pltpu.VMEM((UNITS, HD, 4 * ROWS), BF16),
            pltpu.VMEM((UNITS, ROWS, HD), BF16),
            pltpu.VMEM((4, UNITS, ROWS, HD), BF16),
            pltpu.VMEM((CHIPS,) + block, F32),
            pltpu.VMEM((CHIPS, CHUNKS, 8, HD), F32),
            pltpu.VMEM((2, CHIPS) + block, BF16),
            pltpu.VMEM((2, CHIPS, CHUNKS, 8, HD), F32),
            pltpu.VMEM((CHIPS,) + block, BF16),
            pltpu.VMEM((CHIPS, CHUNKS, 8, HD), F32),
            pltpu.VMEM(block, BF16),
            pltpu.VMEM((2, 2 * HEADS_CORE, ROWS, HD), BF16),
            pltpu.VMEM((2, 2, ROWS, width // 2), BF16),
            pltpu.VMEM((2, 2, ROWS, width // 2), BF16),
            pltpu.VMEM((2, ROWS, width), F32),
            pltpu.VMEM((2, ROWS, width // 2), BF16),
            pltpu.VMEM((2, ROWS, width // 2), BF16),
            dma, dma,
            dma((5,)), dma((5,)),
            dma((2, CHIPS, CHUNKS)), dma((CHIPS, CHUNKS)),
            dma((CHIPS, CHUNKS)), dma((2, CHIPS, CHUNKS)),
            dma((CHIPS, CHUNKS)), dma((2, CHIPS, CHUNKS)),
            dma((CHUNKS,)), dma((CHUNKS,)),
            dma((2, 2)), dma((2, 2)),
            dma((2,)), dma((2,)),
        ],
        compiler_params=pltpu.CompilerParams(
            collective_id=0, has_side_effects=True, vmem_limit_bytes=60 * 2**20
        ),
        name="fused_step",
    )(
        img_hidden, img_query, img_key, img_value, txt_key, txt_value,
        query_gain.reshape(1, HD), key_gain, gate, proj_weight, proj_bias.reshape(1, width),
        guidance, text_len,
        jnp.asarray(rope_table(2 * CHIPS)), jnp.asarray(swap_matrix(), BF16),
    )
    index = step_index[0]
    u_now = 1.0 - index.astype(F32) / STEPS
    u_next = 1.0 - (index + 1).astype(F32) / STEPS
    step_size = 3.0 * u_next / (1.0 + 2.0 * u_next) - 3.0 * u_now / (1.0 + 2.0 * u_now)
    next_state = (latent.astype(F32) + step_size * guided_f).astype(BF16)
    return (guided_f.astype(BF16), next_state)


def fits_fused(mesh):
    return mesh.shape["seq"] == 2 * CHIPS and mesh.shape["blk"] == 2 and mesh.shape["guide"] == 2


def solution(mesh):
    return jax.shard_map(
        fused_shards if fits_fused(mesh) else shards,
        mesh=mesh,
        in_specs=(
            P("guide", None, "seq", "blk"),
            P("guide", None, "seq", "blk"),
            P("guide", None, "seq", "blk"),
            P("guide", None, "seq", "blk"),
            P("guide", None, "seq", "blk"),
            P("guide", None, "seq", "blk"),
            P(),
            P(),
            P("guide", None, "blk"),
            P("blk", None),
            P("blk"),
            P(),
            P(),
            P(),
            P("guide", "seq", "blk"),
        ),
        out_specs=(P("guide", "seq", "blk"), P("guide", "seq", "blk")),
        check_vma=False,
    )
```
